256 devices in a mesh: rep: 2 (over x_lo), row: 8 (over y, core), col: 16 (over x_hi, z).
Axes of the slice: x: 4 (x_hi: 2, x_lo: 2; x = x_hi * 2 + x_lo), y: 4, z: 8, core: 2. Of those that a mesh axis runs over, the one named last changes fastest.
Arguments:
- pre_act: bfloat16 [2048, 24576], P(('rep', 'row'), 'col'), may hold values from -8 to 8
- out_grad: bfloat16 [2048, 12288], P(('rep', 'col'), 'row'), may hold values from -1.25 to 1.25
- down_weight: bfloat16 [12288, 24576], P('row', 'col'), may hold values from -0.0546875 to 0.0546875
Outputs:
- pre_grad: bfloat16 [2048, 24576], P(('rep', 'row'), 'col')
- weight_grad: bfloat16 [12288, 24576], P('row', 'col')
The draws below stay inside these ranges and needn't reach their ends.
All inputs are finite; a program needn't handle non-finite values.
Results may differ from the reference program's by a relative error of at most 0.0048.
Values may be sent and summed in bfloat16 or wider, within the bound.
No kernel may reach another device: no remote copies, remote signals or barrier semaphores. Data moves between devices by JAX's collectives and lax.ppermute only.
A program may use at most 128 MiB of HBM per device.

```python
import jax
import jax.numpy as jnp
from jax import lax

D = 12288
FF = 24576
TOKENS = 2048


def steps_of(stream_key, extent, shards, low, largest):
    factor_of = 1.0
    for dim, blocks in shards:
        heights = jax.random.uniform(jax.random.fold_in(jax.random.fold_in(stream_key, 6), dim), (blocks,), jnp.float32, low / len(shards), largest / len(shards))
        factor_of = factor_of * jnp.repeat(jnp.exp(heights), extent[dim] // blocks).reshape((-1,) + (1,) * (len(extent) - 1 - dim))
    return factor_of


def normal_values(stream_key, shape, deviation, most, shards=(), dtype=jnp.bfloat16):
    factor_of = steps_of(stream_key, shape, shards, -0.22, 0.18) if shards else 1.0
    values = jax.random.normal(stream_key, shape, jnp.float32) * deviation * factor_of
    return jnp.minimum(jnp.maximum(values, -most), most).astype(dtype)


def setup_inputs(seed: int = 0) -> dict:
    splits = jax.random.split(jax.random.key(seed), 4)
    return {
        "pre_act": normal_values(splits[0], (TOKENS, FF), 1.5, 8.0, ((0, 16), (1, 16))),
        "out_grad": normal_values(splits[1], (TOKENS, D), 0.2, 1.25, ((0, 32), (1, 8))),
        "down_weight": normal_values(splits[2], (D, FF), D ** -0.5, 0.0546875, ((0, 8), (1, 16))),
    }


root_coef = 0.7978845608
cube_coef = 0.044715


def gelu_tanh(value):
    inner = jnp.tanh(root_coef * (value + cube_coef * value * value * value))
    return 0.5 * value * (1.0 + inner)


def gelu_slope(value):
    inner = jnp.tanh(root_coef * (value + cube_coef * value * value * value))
    return 0.5 * (1.0 + inner) + 0.5 * value * (1.0 - inner * inner) * root_coef * (1.0 + 3.0 * cube_coef * value * value)


def reference(pre_act, out_grad, down_weight):
    pre_wide = pre_act.astype(jnp.float32)
    activation = gelu_tanh(pre_wide).astype(jnp.bfloat16)
    grad_act = jnp.dot(out_grad, down_weight, preferred_element_type=jnp.float32)
    pre_grad = (grad_act * gelu_slope(pre_wide)).astype(jnp.bfloat16)
    weight_grad = lax.dot_general(out_grad, activation, (((0,), (0,)), ((), ())), preferred_element_type=jnp.float32)
    return pre_grad, weight_grad.astype(jnp.bfloat16)
```

```python
import jax
import jax.numpy as jnp
from jax import lax
from jax.experimental import pallas as pl
from jax.experimental.pallas import tpu as pltpu
from jax.sharding import Mesh, PartitionSpec as P

root_coef = 0.7978845608
cube_coef = 0.044715

XL, Y, C, XH, Z = 2, 4, 2, 2, 8
AXES = ("xl", "y", "c", "xh", "z")
HALF = 32
BF, F32 = jnp.bfloat16, jnp.float32
ANY = pl.BlockSpec(memory_space=pl.ANY)


def gelu_tanh(value):
    inner = jnp.tanh(root_coef * (value + cube_coef * value * value * value))
    return 0.5 * value * (1.0 + inner)


def gelu_slope(value):
    inner = jnp.tanh(root_coef * (value + cube_coef * value * value * value))
    return 0.5 * (1.0 + inner) + 0.5 * value * (1.0 - inner * inner) * root_coef * (
        1.0 + 3.0 * cube_coef * value * value
    )


def along_z(a, d):
    return lax.ppermute(a, "z", [(i, (i + d) % Z) for i in range(Z)])


def along_x(a, d):
    def place(x):
        return (x % 2) * XH + x // 2

    return lax.ppermute(a, ("xl", "xh"), [(place(x), place((x + d) % 4)) for x in range(4)])


def along_y(a, d):
    return lax.ppermute(a, "y", [(i, (i + d) % Y) for i in range(Y)])


def round_y(a):
    pairs = [((y, c), ((y + (1 if c == 0 else -1)) % Y, c)) for y in range(Y) for c in range(C)]
    return lax.ppermute(a, ("y", "c"), [(s[0] * C + s[1], t[0] * C + t[1]) for s, t in pairs])


def swap(a, axis):
    return lax.ppermute(a, axis, [(0, 1), (1, 0)])


def rows(offset, count):
    return pl.ds(pl.multiple_of(offset, count), count)


def place_all(moves, whole, sem):
    for source, target in moves:
        pltpu.make_async_copy(source, target, sem).start()
    for source, target in moves:
        pltpu.make_async_copy(source, target, sem).wait()


def grad_moves(ring, cols, relay_a, relay_b, spot, replicas):
    z = lax.axis_index("z")
    moves = []
    for j in range(8):
        zp = lax.rem(z + 8 - j, 8)
        ref = ring[j]
        order = (0, 2, 3, 1) if replicas else (0, 2)
        first, second = ref if isinstance(ref, tuple) else (ref, None)
        sources = [first.at[pl.ds(0, 32)], first.at[pl.ds(32, 32)]]
        if replicas and second is not None:
            sources += [second.at[pl.ds(0, 32)], second.at[pl.ds(32, 32)]]
        elif replicas:
            sources += [first.at[pl.ds(64, 32)], first.at[pl.ds(96, 32)]]
        for k, dx in enumerate(order):
            moves.append((sources[k], spot(dx, zp, 0)))
        for dx, ref in cols:
            moves.append((ref.at[pl.ds(32 * j, 32)], spot(dx, zp, 1)))
        ref = relay_a if j < 4 else relay_b
        moves.append((ref.at[pl.ds(32 * (j % 4), 32)], spot(2, zp, 1)))
    return moves


def partial_kernel(*refs):
    ring = list(refs[:8])
    col, relay_a, relay_b, w_ref, mine_ref, other_ref, held, sem = refs[8:]
    y, c, xh = lax.axis_index("y"), lax.axis_index("c"), lax.axis_index("xh")

    def spot(dx, zp, half):
        xp = xh if dx == 0 else 1 - xh
        yp, cp = 2 * xp + zp // 4, lax.rem(zp // 2, 2)
        away = lax.rem(cp + c, 2)
        return held.at[rows(away * 512 + lax.rem(yp + 4 - y, 4) * 128 + lax.rem(zp, 2) * 64 + half * 32, 32)]

    @pl.when(pl.program_id(0) == 0)
    def _():
        place_all(grad_moves(ring, [(0, col)], relay_a, relay_b, spot, False), held, sem)

    other_ref[...] = jnp.dot(held[512:, :], w_ref[...], preferred_element_type=F32).astype(BF)
    mine_ref[...] = jnp.dot(held[:512, :], w_ref[...], preferred_element_type=F32)


def partial_grad(ring, col, relay_a, relay_b, weight):
    step = 256
    return pl.pallas_call(
        partial_kernel,
        grid=(1536 // step,),
        in_specs=[ANY] * 11 + [pl.BlockSpec((1536, step), lambda n: (0, n))],
        out_specs=[pl.BlockSpec((512, step), lambda n: (0, n))] * 2,
        out_shape=[jax.ShapeDtypeStruct((512, 1536), F32), jax.ShapeDtypeStruct((512, 1536), BF)],
        scratch_shapes=[pltpu.VMEM((1024, 1536), BF), pltpu.SemaphoreType.DMA],
        compiler_params=pltpu.CompilerParams(vmem_limit_bytes=40 << 20),
        cost_estimate=pl.CostEstimate(flops=2 * 1024 * 1536 * 1536, bytes_accessed=13 << 20, transcendentals=0),
    )(*ring, col, relay_a, relay_b, weight)


def weight_kernel(*refs):
    ring = list(refs[:7]) + [(refs[7], refs[8])]
    ring = ring[:4] + [ring[7]] + ring[4:7]
    col, left, right, relay_a, relay_b, own, swapped = refs[9:16]
    out_ref, grads, acts, sem = refs[16:]
    y, c, xl, xh = (lax.axis_index(a) for a in ("y", "c", "xl", "xh"))
    x = 2 * xh + xl

    def spot(dx, zp, half):
        xp = lax.rem(x + dx, 4)
        return grads.at[rows(lax.rem(xp, 2) * 1024 + (xp // 2) * 512 + zp * 64 + half * 32, 32)]

    def act_spot(other_rep, yp, cp):
        rep = 1 - xl if other_rep else xl
        return acts.at[rows(rep * 1024 + (lax.rem(yp + 4, 4) * 2 + cp) * 128, 128)]

    @pl.when(pl.program_id(0) == 0)
    def _():
        moves = grad_moves(ring, [(0, col), (3, left), (1, right)], relay_a, relay_b, spot, True)
        back = 2 * c - 1
        for ref, owner, ahead in ((own, c, back), (swapped, 1 - c, -back)):
            if ref is own:
                spots = [(0, c), (0, 1 - c), (ahead, c), (ahead, 1 - c), (2, c)]
            else:
                spots = [(ahead, 1 - c), (ahead, c), (2, 1 - c)]
            for k, (dy, cp) in enumerate(spots):
                for other in range(2):
                    moves.append((ref.at[pl.ds(256 * k + 128 * other, 128)], act_spot(other, y + dy, cp)))
        place_all(moves, grads, sem)

    lanes = pl.ds(pl.multiple_of(pl.program_id(0) * 256, 256), 256)
    out_ref[...] = lax.dot_general(
        grads[:, lanes], acts[...], (((0,), (0,)), ((), ())), preferred_element_type=F32
    ).astype(BF)


def weight_gradient(*arrays):
    step = 256
    return pl.pallas_call(
        weight_kernel,
        grid=(1536 // step,),
        in_specs=[ANY] * len(arrays),
        out_specs=pl.BlockSpec((step, 1536), lambda m: (m, 0)),
        out_shape=jax.ShapeDtypeStruct((1536, 1536), BF),
        scratch_shapes=[pltpu.VMEM((2048, 1536), BF), pltpu.VMEM((2048, 1536), BF), pltpu.SemaphoreType.DMA],
        compiler_params=pltpu.CompilerParams(vmem_limit_bytes=48 << 20),
        cost_estimate=pl.CostEstimate(flops=2 * 2048 * 1536 * 1536, bytes_accessed=17 << 20, transcendentals=0),
    )(*arrays)


def per_device(pre_act, out_grad, down_weight):
    pre_wide = pre_act.astype(F32)
    first, second = out_grad[:HALF], out_grad[HALF:]

    activation = gelu_tanh(pre_wide).astype(BF)
    two = jnp.concatenate([activation, swap(activation, "xl")])
    chip = jnp.concatenate([two, swap(two, "c")])
    near = round_y(chip)
    far = round_y(near[:256])
    came = jnp.concatenate([near, far])
    own_acts = jnp.concatenate([chip, came])
    swapped_acts = swap(came, "c")

    x_left, x_right = along_x(first, 1), along_x(first, -1)
    x_far = [along_x(x_left[:16], 1), along_x(x_right[16:], -1)]
    bundle = jnp.concatenate([first, *x_far, x_left, x_right])
    up, down = [bundle], [bundle]
    for _ in range(3):
        up.append(along_z(up[-1], 1))
        down.append(along_z(down[-1], -1))
    opposite = (along_z(up[-1][:64], 1), along_z(down[-1][64:], -1))

    z_up, z_down = [second], [second]
    for _ in range(3):
        z_up.append(along_z(z_up[-1], 1))
        z_down.append(along_z(z_down[-1], -1))
    z_far = [along_z(z_up[-1][:16], 1), along_z(z_down[-1][16:], -1)]
    column = jnp.concatenate([*z_up, *z_far, z_down[3], z_down[2], z_down[1]])
    left, right = along_x(column, 1), along_x(column, -1)
    relay_a, relay_b = along_x(left[:128], 1), along_x(right[128:], -1)

    ring = [up[0], up[1], up[2], up[3], opposite[0], down[3], down[2], down[1]]
    mine, other = partial_grad(ring, column, relay_a, relay_b, down_weight)
    other = swap(other, "c")

    def summed(block):
        return mine[128 * block : 128 * block + 128] + other[128 * block : 128 * block + 128].astype(F32)

    across = summed(2).astype(BF)
    from_below, from_above = along_y(across[:64], 1), along_y(across[64:], -1)
    empty = jnp.zeros((64, 1536), F32)
    upward = (summed(1) + jnp.concatenate([from_below.astype(F32), empty])).astype(BF)
    downward = (summed(3) + jnp.concatenate([empty, from_above.astype(F32)])).astype(BF)
    grad_act = summed(0) + along_y(upward, 1).astype(F32) + along_y(downward, -1).astype(F32)
    pre_grad = (grad_act * gelu_slope(pre_wide)).astype(BF)

    weight_grad = weight_gradient(
        up[0], up[1], up[2], up[3], down[3], down[2], down[1], *opposite,
        column, left, right, relay_a, relay_b, own_acts, swapped_acts,
    )
    return (pre_grad, weight_grad)


def solution(mesh):
    physical = Mesh(mesh.devices.reshape(XL, Y, C, XH, Z), AXES)
    rep, row, col = "xl", ("y", "c"), ("xh", "z")
    return jax.shard_map(
        per_device,
        mesh=physical,
        in_specs=(P((rep, *row), col), P((rep, *col), row), P(row, col)),
        out_specs=(P((rep, *row), col), P(row, col)),
        check_vma=False,
    )
```

```python
import jax
import jax.numpy as jnp
from jax import lax
from jax.experimental import pallas as pl
from jax.experimental.pallas import tpu as pltpu
from jax.sharding import Mesh, PartitionSpec as P

root_coef = 0.7978845608
cube_coef = 0.044715

XL, Y, C, XH, Z = 2, 4, 2, 2, 8
AXES = ("xl", "y", "c", "xh", "z")
BF, F32 = jnp.bfloat16, jnp.float32


def gelu_tanh(value):
    inner = jnp.tanh(root_coef * (value + cube_coef * value * value * value))
    return 0.5 * value * (1.0 + inner)


def gelu_slope(value):
    inner = jnp.tanh(root_coef * (value + cube_coef * value * value * value))
    return 0.5 * (1.0 + inner) + 0.5 * value * (1.0 - inner * inner) * root_coef * (
        1.0 + 3.0 * cube_coef * value * value
    )


def along_z(a, d):
    return lax.ppermute(a, "z", [(i, (i + d) % Z) for i in range(Z)])


def along_x(a, d):
    def place(x):
        return (x % 2) * XH + x // 2

    return lax.ppermute(a, ("xl", "xh"), [(place(x), place((x + d) % 4)) for x in range(4)])


def along_y(a, d):
    return lax.ppermute(a, "y", [(i, (i + d) % Y) for i in range(Y)])


def round_y(a):
    pairs = [((y, c), ((y + (1 if c == 0 else -1)) % Y, c)) for y in range(Y) for c in range(C)]
    return lax.ppermute(a, ("y", "c"), [(s[0] * C + s[1], t[0] * C + t[1]) for s, t in pairs])


def swap(a, axis):
    return lax.ppermute(a, axis, [(0, 1), (1, 0)])


def tie(*arrays):
    return lax.optimization_barrier(arrays)


OWN = [0, -1, 1, -2, 2, -3, 3, 4]


def partial_kernel(grads_ref, w_ref, mine_ref, other_ref, held):
    y, c, xh, z = (lax.axis_index(a) for a in ("y", "c", "xh", "z"))
    held_new = jnp.dot(grads_ref[...], w_ref[...], preferred_element_type=F32)
    for k in range(16):
        xp = xh if k < 8 else 1 - xh
        zp = lax.rem(z + OWN[k % 8] + 8, 8)
        yp, cp = 2 * xp + zp // 4, lax.rem(zp // 2, 2)
        spot = lax.rem(cp + c, 2) * 512 + lax.rem(yp + 4 - y, 4) * 128 + lax.rem(zp, 2) * 64
        held[pl.ds(pl.multiple_of(spot, 64), 64), :] = held_new[64 * k : 64 * k + 64]
    mine_ref[...] = held[:512]
    other_ref[...] = held[512:].astype(BF)


def partial_grad(grads, weight):
    step = 512
    return pl.pallas_call(
        partial_kernel,
        grid=(1536 // step,),
        in_specs=[pl.BlockSpec((1024, 1536), lambda n: (0, 0)), pl.BlockSpec((1536, step), lambda n: (0, n))],
        out_specs=[pl.BlockSpec((512, step), lambda n: (0, n))] * 2,
        out_shape=[jax.ShapeDtypeStruct((512, 1536), F32), jax.ShapeDtypeStruct((512, 1536), BF)],
        scratch_shapes=[pltpu.VMEM((1024, step), F32)],
        compiler_params=pltpu.CompilerParams(vmem_limit_bytes=28 << 20),
        cost_estimate=pl.CostEstimate(flops=2 * 1024 * 1536 * 1536, bytes_accessed=13 << 20, transcendentals=0),
    )(grads, weight)


def weight_kernel(grads_ref, acts_ref, out_ref, acts):
    y, c, xl, xh, z = (lax.axis_index(a) for a in ("y", "c", "xl", "xh", "z"))

    @pl.when(pl.program_id(0) == 0)
    def _():
        for k in range(32):
            dx = (0, 2, 3, 1)[k // 8]
            xp = lax.rem(2 * xh + xl + dx, 4)
            zp = lax.rem(z + OWN[k % 8] + 8, 8)
            dy = lax.rem(2 * (xp // 2) + zp // 4 + 4 - y, 4)
            away = lax.rem(lax.rem(zp // 2, 2) + c, 2)
            back = jnp.where(c == 0, 3, 1)
            block = jnp.where(
                dy == 0, away, jnp.where(dy == 2, 4 + 3 * away, jnp.where(dy == back, 2 + away, 6 - away))
            )
            start = block * 256 + (dx % 2) * 128 + lax.rem(zp, 2) * 64
            acts[64 * k : 64 * k + 64, :] = acts_ref[pl.ds(pl.multiple_of(start, 64), 64), :]

    out_ref[...] = lax.dot_general(
        grads_ref[...], acts[...], (((0,), (0,)), ((), ())), preferred_element_type=F32
    ).astype(BF)


def weight_gradient(grads, acts):
    step = 256
    return pl.pallas_call(
        weight_kernel,
        grid=(1536 // step,),
        in_specs=[pl.BlockSpec((2048, step), lambda m: (0, m)), pl.BlockSpec((2048, 1536), lambda m: (0, 0))],
        out_specs=pl.BlockSpec((step, 1536), lambda m: (m, 0)),
        out_shape=jax.ShapeDtypeStruct((1536, 1536), BF),
        scratch_shapes=[pltpu.VMEM((2048, 1536), BF)],
        compiler_params=pltpu.CompilerParams(vmem_limit_bytes=36 << 20),
        cost_estimate=pl.CostEstimate(flops=2 * 2048 * 1536 * 1536, bytes_accessed=17 << 20, transcendentals=0),
    )(grads, acts)


def per_device(pre_act, out_grad, down_weight):
    pre_wide = pre_act.astype(F32)
    g = out_grad
    activation = gelu_tanh(pre_wide).astype(BF)

    up1, down1, far = along_z(g, 1), along_z(g, -1), along_x(g, 2)
    other_rep = swap(activation, "xl")
    up1, down1, far, other_rep = tie(up1, down1, far, other_rep)

    up2 = along_z(jnp.concatenate([far, up1]), 1)
    down2 = along_z(jnp.concatenate([down1, far]), -1)
    near = jnp.concatenate([g, up1, down1])
    left_a, right_a = along_x(near, 1), along_x(near, -1)
    two = jnp.concatenate([activation, other_rep])
    two_c = swap(two, "c")
    up2, down2, left_a, right_a, two_c = tie(up2, down2, left_a, right_a, two_c)

    up3, down3 = along_z(up2, 1), along_z(down2, -1)
    pair = jnp.concatenate([up2[64:], down2[:64]])
    left_b, right_b = along_x(pair, 1), along_x(pair, -1)
    acts_1 = round_y(jnp.concatenate([two, two_c]))
    up3, down3, left_b, right_b, acts_1 = tie(up3, down3, left_b, right_b, acts_1)

    up4, down4 = along_z(up3[:96], 1), along_z(down3[32:], -1)
    pair = jnp.concatenate([up3[64:], down3[:64]])
    left_c, right_c = along_x(pair, 1), along_x(pair, -1)
    acts_2 = round_y(acts_1[:256])
    up4, down4, left_c, right_c, acts_2 = tie(up4, down4, left_c, right_c, acts_2)

    up5, down5 = along_z(up4[:32], 1), along_z(down4[64:], -1)
    last = jnp.concatenate([up4[64:], down4[:32]])
    left_d, right_d = along_x(last, 1), along_x(last, -1)
    came = jnp.concatenate([acts_1, acts_2])
    swapped = swap(came, "c")

    own = [g, up1, down1, up2[64:], down2[:64], up3[64:], down3[:64], last]
    second = [far, up2[:64], down2[64:], up3[:64], down3[64:], up4[:64], down4[32:], up5, down5]
    grads_own = jnp.concatenate(own + second)

    mine, other = partial_grad(grads_own, down_weight)
    other = swap(other, "c")
    _, left_d, right_d, swapped = tie(other, left_d, right_d, swapped)

    def summed(block):
        return mine[128 * block : 128 * block + 128] + other[128 * block : 128 * block + 128].astype(F32)

    from_below = along_y(summed(1).astype(BF), 1)
    from_above = along_y(summed(3).astype(BF), -1)
    from_across = along_y(summed(2).astype(BF), 2)
    grad_act = summed(0) + from_below.astype(F32) + from_above.astype(F32) + from_across.astype(F32)
    pre_grad = (grad_act * gelu_slope(pre_wide)).astype(BF)

    grads = jnp.concatenate([grads_own, left_a, left_b, left_c, left_d, right_a, right_b, right_c, right_d])
    acts = jnp.concatenate([two, two_c, came, swapped])
    weight_grad = weight_gradient(grads, acts)
    return (pre_grad, weight_grad)


def solution(mesh):
    physical = Mesh(mesh.devices.reshape(XL, Y, C, XH, Z), AXES)
    rep, row, col = "xl", ("y", "c"), ("xh", "z")
    return jax.shard_map(
        per_device,
        mesh=physical,
        in_specs=(P((rep, *row), col), P((rep, *col), row), P(row, col)),
        out_specs=(P((rep, *row), col), P(row, col)),
        check_vma=False,
    )
```

```python
import jax
import jax.numpy as jnp
from jax import lax
from jax.experimental import pallas as pl
from jax.experimental.pallas import tpu as pltpu
from jax.sharding import Mesh, PartitionSpec as P

root_coef = 0.7978845608
cube_coef = 0.044715

XL, Y, C, XH, Z = 2, 4, 2, 2, 8
AXES = ("xl", "y", "c", "xh", "z")
BF, F32 = jnp.bfloat16, jnp.float32


def gelu_tanh(value):
    inner = jnp.tanh(root_coef * (value + cube_coef * value * value * value))
    return 0.5 * value * (1.0 + inner)


def gelu_slope(value):
    inner = jnp.tanh(root_coef * (value + cube_coef * value * value * value))
    return 0.5 * (1.0 + inner) + 0.5 * value * (1.0 - inner * inner) * root_coef * (
        1.0 + 3.0 * cube_coef * value * value
    )


def along_z(a, d):
    return lax.ppermute(a, "z", [(i, (i + d) % Z) for i in range(Z)])


def along_x(a, d):
    def place(x):
        return (x % 2) * XH + x // 2

    return lax.ppermute(a, ("xl", "xh"), [(place(x), place((x + d) % 4)) for x in range(4)])


def along_y(a, d):
    return lax.ppermute(a, "y", [(i, (i + d) % Y) for i in range(Y)])


def round_y(a):
    pairs = [((y, c), ((y + (1 if c == 0 else -1)) % Y, c)) for y in range(Y) for c in range(C)]
    return lax.ppermute(a, ("y", "c"), [(s[0] * C + s[1], t[0] * C + t[1]) for s, t in pairs])


def swap(a, axis):
    return lax.ppermute(a, axis, [(0, 1), (1, 0)])


def tie(*arrays):
    return lax.optimization_barrier(arrays)


OWN = [0, -1, 1, -2, 2, -3, 3, 4]


def partial_kernel(grads_ref, w_ref, mine_ref, other_ref, held):
    y, c, xh, z = (lax.axis_index(a) for a in ("y", "c", "xh", "z"))
    held_new = jnp.dot(grads_ref[...], w_ref[...], preferred_element_type=F32)
    for k in range(16):
        xp = xh if k < 8 else 1 - xh
        zp = lax.rem(z + OWN[k % 8] + 8, 8)
        yp, cp = 2 * xp + zp // 4, lax.rem(zp // 2, 2)
        spot = lax.rem(cp + c, 2) * 512 + lax.rem(yp + 4 - y, 4) * 128 + lax.rem(zp, 2) * 64
        held[pl.ds(pl.multiple_of(spot, 64), 64), :] = held_new[64 * k : 64 * k + 64]
    mine_ref[...] = held[:512]
    other_ref[...] = held[512:].astype(BF)


def partial_grad(grads, weight):
    step = 512
    return pl.pallas_call(
        partial_kernel,
        grid=(1536 // step,),
        in_specs=[pl.BlockSpec((1024, 1536), lambda n: (0, 0)), pl.BlockSpec((1536, step), lambda n: (0, n))],
        out_specs=[pl.BlockSpec((512, step), lambda n: (0, n))] * 2,
        out_shape=[jax.ShapeDtypeStruct((512, 1536), F32), jax.ShapeDtypeStruct((512, 1536), BF)],
        scratch_shapes=[pltpu.VMEM((1024, step), F32)],
        compiler_params=pltpu.CompilerParams(vmem_limit_bytes=28 << 20),
        cost_estimate=pl.CostEstimate(flops=2 * 1024 * 1536 * 1536, bytes_accessed=13 << 20, transcendentals=0),
    )(grads, weight)


def weight_kernel(grads_ref, acts_ref, out_ref, acts):
    y, c, xl, xh, z = (lax.axis_index(a) for a in ("y", "c", "xl", "xh", "z"))

    @pl.when(pl.program_id(0) == 0)
    def _():
        for k in range(32):
            dx = (0, 2, 3, 1)[k // 8]
            xp = lax.rem(2 * xh + xl + dx, 4)
            zp = lax.rem(z + OWN[k % 8] + 8, 8)
            dy = lax.rem(2 * (xp // 2) + zp // 4 + 4 - y, 4)
            away = lax.rem(lax.rem(zp // 2, 2) + c, 2)
            back = jnp.where(c == 0, 3, 1)
            other = dx % 2
            block = jnp.where(
                dy == 0,
                2 * other + away,
                3 * other
                + jnp.where(dy == 2, 6 + 6 * away, jnp.where(dy == back, 4 + away, 11 - away)),
            )
            start = block * 128 + lax.rem(zp, 2) * 64
            acts[64 * k : 64 * k + 64, :] = acts_ref[pl.ds(pl.multiple_of(start, 64), 64), :]

    out_ref[...] = lax.dot_general(
        grads_ref[...], acts[...], (((0,), (0,)), ((), ())), preferred_element_type=F32
    ).astype(BF)


def weight_gradient(grads, acts):
    step = 256
    return pl.pallas_call(
        weight_kernel,
        grid=(1536 // step,),
        in_specs=[pl.BlockSpec((2048, step), lambda m: (0, m)), pl.BlockSpec((2048, 1536), lambda m: (0, 0))],
        out_specs=pl.BlockSpec((step, 1536), lambda m: (m, 0)),
        out_shape=jax.ShapeDtypeStruct((1536, 1536), BF),
        scratch_shapes=[pltpu.VMEM((2048, 1536), BF)],
        compiler_params=pltpu.CompilerParams(vmem_limit_bytes=36 << 20),
        cost_estimate=pl.CostEstimate(flops=2 * 2048 * 1536 * 1536, bytes_accessed=17 << 20, transcendentals=0),
    )(grads, acts)


def per_device(pre_act, out_grad, down_weight):
    pre_wide = pre_act.astype(F32)
    g = out_grad
    activation = gelu_tanh(pre_wide).astype(BF)

    up1, down1, far = along_z(g, 1), along_z(g, -1), along_x(g, 2)
    act_c = swap(activation, "c")
    activation, act_c, up1, down1, far = tie(activation, act_c, up1, down1, far)

    up2 = along_z(jnp.concatenate([far, up1]), 1)
    down2 = along_z(jnp.concatenate([down1, far]), -1)
    other_rep = swap(activation, "xl")
    chip = jnp.concatenate([activation, act_c])
    hop_1 = round_y(chip)
    up2, down2, other_rep, hop_1 = tie(up2, down2, other_rep, hop_1)

    up3, down3 = along_z(up2, 1), along_z(down2, -1)
    near = jnp.concatenate([g, up1, down1])
    left_a, right_a = along_x(near, 1), along_x(near, -1)
    other_chip = jnp.concatenate([other_rep, swap(other_rep, "c")])
    hop_2 = round_y(jnp.concatenate([hop_1[:128], other_chip]))
    up3, down3, left_a, right_a, other_chip = tie(up3, down3, left_a, right_a, other_chip)

    up4, down4 = along_z(up3[:96], 1), along_z(down3[32:], -1)
    middle = jnp.concatenate([up2[64:], down2[:64]])
    left_b, right_b = along_x(middle, 1), along_x(middle, -1)
    up4, down4, hop_2, left_b, right_b = tie(up4, down4, hop_2, left_b, right_b)

    up5, down5 = along_z(up4[:32], 1), along_z(down4[64:], -1)
    last = jnp.concatenate([up4[64:], down4[:32]])
    hop_3 = round_y(hop_2[128:256])
    up5, down5, hop_3 = tie(up5, down5, hop_3)

    own = [g, up1, down1, up2[64:], down2[:64], up3[64:], down3[:64], last]
    second = [far, up2[:64], down2[64:], up3[:64], down3[64:], up4[:64], down4[32:], up5, down5]
    grads_own = jnp.concatenate(own + second)

    mine, other = partial_grad(grads_own, down_weight)
    other = swap(other, "c")
    third = jnp.concatenate([up3[64:], down3[:64], last])
    left_c, right_c = along_x(third, 1), along_x(third, -1)
    came = jnp.concatenate([hop_1, hop_2, hop_3])
    swapped = swap(came, "c")

    def summed(block):
        return mine[128 * block : 128 * block + 128] + other[128 * block : 128 * block + 128].astype(F32)

    to_above, to_below, to_across = summed(1).astype(BF), summed(3).astype(BF), summed(2).astype(BF)
    to_above, to_below, to_across, swapped = tie(to_above, to_below, to_across, swapped)
    from_across = along_y(to_across, 2)
    from_below, from_above = along_y(to_above, 1), along_y(to_below, -1)

    grads = jnp.concatenate([grads_own, left_a, left_b, left_c, right_a, right_b, right_c])
    acts = jnp.concatenate([chip, other_chip, came, swapped])
    weight_grad = weight_gradient(grads, acts)
    from_across, from_below, from_above, weight_grad = tie(from_across, from_below, from_above, weight_grad)
    grad_act = summed(0) + from_below.astype(F32) + from_above.astype(F32) + from_across.astype(F32)
    pre_grad = (grad_act * gelu_slope(pre_wide)).astype(BF)
    return (pre_grad, weight_grad)


def solution(mesh):
    physical = Mesh(mesh.devices.reshape(XL, Y, C, XH, Z), AXES)
    rep, row, col = "xl", ("y", "c"), ("xh", "z")
    return jax.shard_map(
        per_device,
        mesh=physical,
        in_specs=(P((rep, *row), col), P((rep, *col), row), P(row, col)),
        out_specs=(P((rep, *row), col), P(row, col)),
        check_vma=False,
    )
```

```python
import jax
import jax.numpy as jnp
from jax import lax
from jax.experimental import pallas as pl
from jax.experimental.pallas import tpu as pltpu
from jax.sharding import Mesh, PartitionSpec as P

root_coef = 0.7978845608
cube_coef = 0.044715

XL, Y, C, XH, Z = 2, 4, 2, 2, 8
AXES = ("xl", "y", "c", "xh", "z")
BF, F32 = jnp.bfloat16, jnp.float32


def gelu_tanh(value):
    inner = jnp.tanh(root_coef * (value + cube_coef * value * value * value))
    return 0.5 * value * (1.0 + inner)


def gelu_slope(value):
    inner = jnp.tanh(root_coef * (value + cube_coef * value * value * value))
    return 0.5 * (1.0 + inner) + 0.5 * value * (1.0 - inner * inner) * root_coef * (
        1.0 + 3.0 * cube_coef * value * value
    )


def along_z(a, d):
    return lax.ppermute(a, "z", [(i, (i + d) % Z) for i in range(Z)])


def along_x(a, d):
    def place(x):
        return (x % 2) * XH + x // 2

    return lax.ppermute(a, ("xl", "xh"), [(place(x), place((x + d) % 4)) for x in range(4)])


def along_y(a, d):
    return lax.ppermute(a, "y", [(i, (i + d) % Y) for i in range(Y)])


def round_y(a):
    pairs = [((y, c), ((y + (1 if c == 0 else -1)) % Y, c)) for y in range(Y) for c in range(C)]
    return lax.ppermute(a, ("y", "c"), [(s[0] * C + s[1], t[0] * C + t[1]) for s, t in pairs])


def swap(a, axis):
    return lax.ppermute(a, axis, [(0, 1), (1, 0)])


def tie(*arrays):
    return lax.optimization_barrier(arrays)


OWN = [0, -1, 1, -2, 2, -3, 3, 4]


VMEM = pl.BlockSpec(memory_space=pltpu.VMEM)
EARLY = [(0, k) for k in range(7)] + [(1, k) for k in range(5)]
LATE = [(0, 7), (1, 5), (1, 6), (1, 7)]


def early_kernel(grads_ref, w_ref, out_ref):
    out_ref[...] = jnp.dot(grads_ref[...], w_ref[...], preferred_element_type=F32)


def early_partial(grads, weight):
    step = 512
    count = 64 * len(EARLY)
    return pl.pallas_call(
        early_kernel,
        grid=(1536 // step,),
        in_specs=[pl.BlockSpec((count, 1536), lambda n: (0, 0)), pl.BlockSpec((1536, step), lambda n: (0, n))],
        out_specs=pl.BlockSpec((count, step), lambda n: (0, n)),
        out_shape=jax.ShapeDtypeStruct((count, 1536), F32),
        compiler_params=pltpu.CompilerParams(vmem_limit_bytes=24 << 20),
        cost_estimate=pl.CostEstimate(flops=2 * count * 1536 * 1536, bytes_accessed=12 << 20, transcendentals=0),
    )(grads, weight)


def late_kernel(early_ref, grads_ref, w_ref, mine_ref, other_ref, late):
    y, c, xh, z = (lax.axis_index(a) for a in ("y", "c", "xh", "z"))

    def place(source, which):
        for k, (far, j) in enumerate(which):
            xp = 1 - xh if far else xh
            zp = lax.rem(z + OWN[j] + 8, 8)
            yp, cp = 2 * xp + zp // 4, lax.rem(zp // 2, 2)
            start = pl.multiple_of(lax.rem(yp + 4 - y, 4) * 128 + lax.rem(zp, 2) * 64, 64)

            @pl.when(cp == c)
            def _():
                mine_ref[pl.ds(start, 64), :] = source[64 * k : 64 * k + 64, :]

            @pl.when(cp != c)
            def _():
                other_ref[pl.ds(start, 64), :] = source[64 * k : 64 * k + 64, :].astype(BF)

    for n in range(3):
        late[:, 512 * n : 512 * n + 512] = jnp.dot(
            grads_ref[...], w_ref[:, 512 * n : 512 * n + 512], preferred_element_type=F32
        )
    place(early_ref, EARLY)
    place(late, LATE)


def late_partial(early, grads, weight):
    return pl.pallas_call(
        late_kernel,
        in_specs=[VMEM] * 3,
        out_specs=[VMEM] * 2,
        out_shape=[jax.ShapeDtypeStruct((512, 1536), F32), jax.ShapeDtypeStruct((512, 1536), BF)],
        scratch_shapes=[pltpu.VMEM((256, 1536), F32)],
        compiler_params=pltpu.CompilerParams(vmem_limit_bytes=32 << 20),
        cost_estimate=pl.CostEstimate(flops=2 * 256 * 1536 * 1536, bytes_accessed=8 << 20, transcendentals=0),
    )(early, grads, weight)


def weight_kernel(grads_ref, acts_ref, out_ref, acts):
    y, c, xl, xh, z = (lax.axis_index(a) for a in ("y", "c", "xl", "xh", "z"))

    @pl.when(pl.program_id(0) == 0)
    def _():
        for k in range(32):
            dx = (0, 2, 3, 1)[k // 8]
            xp = lax.rem(2 * xh + xl + dx, 4)
            zp = lax.rem(z + OWN[k % 8] + 8, 8)
            dy = lax.rem(2 * (xp // 2) + zp // 4 + 4 - y, 4)
            away = lax.rem(lax.rem(zp // 2, 2) + c, 2)
            back = jnp.where(c == 0, 3, 1)
            other = dx % 2
            block = jnp.where(
                dy == 0,
                2 * other + away,
                3 * other
                + jnp.where(dy == 2, 6 + 6 * away, jnp.where(dy == back, 4 + away, 11 - away)),
            )
            start = block * 128 + lax.rem(zp, 2) * 64
            acts[64 * k : 64 * k + 64, :] = acts_ref[pl.ds(pl.multiple_of(start, 64), 64), :]

    out_ref[...] = lax.dot_general(
        grads_ref[...], acts[...], (((0,), (0,)), ((), ())), preferred_element_type=F32
    ).astype(BF)


def weight_gradient(grads, acts):
    step = 256
    return pl.pallas_call(
        weight_kernel,
        grid=(1536 // step,),
        in_specs=[pl.BlockSpec((2048, step), lambda m: (0, m)), pl.BlockSpec((2048, 1536), lambda m: (0, 0))],
        out_specs=pl.BlockSpec((step, 1536), lambda m: (m, 0)),
        out_shape=jax.ShapeDtypeStruct((1536, 1536), BF),
        scratch_shapes=[pltpu.VMEM((2048, 1536), BF)],
        compiler_params=pltpu.CompilerParams(vmem_limit_bytes=36 << 20),
        cost_estimate=pl.CostEstimate(flops=2 * 2048 * 1536 * 1536, bytes_accessed=17 << 20, transcendentals=0),
    )(grads, acts)


def per_device(pre_act, out_grad, down_weight):
    pre_wide = pre_act.astype(F32)
    g = out_grad
    activation = gelu_tanh(pre_wide).astype(BF)

    up1, down1, far = along_z(g, 1), along_z(g, -1), along_x(g, 2)
    act_c = swap(activation, "c")
    activation, act_c, up1, down1, far = tie(activation, act_c, up1, down1, far)

    up2 = along_z(jnp.concatenate([far, up1]), 1)
    down2 = along_z(jnp.concatenate([down1, far]), -1)
    other_rep = swap(activation, "xl")
    chip = jnp.concatenate([activation, act_c])
    hop_1 = round_y(chip)
    up2, down2, other_rep, hop_1 = tie(up2, down2, other_rep, hop_1)

    up3, down3 = along_z(up2, 1), along_z(down2, -1)
    near = jnp.concatenate([g, up1, down1])
    left_a, right_a = along_x(near, 1), along_x(near, -1)
    other_chip = jnp.concatenate([other_rep, swap(other_rep, "c")])
    hop_2 = round_y(hop_1[:128])
    up3, down3, left_a, right_a, other_chip, hop_2 = tie(up3, down3, left_a, right_a, other_chip, hop_2)

    up4, down4 = along_z(up3[:96], 1), along_z(down3[32:], -1)
    middle = jnp.concatenate([up2[64:], down2[:64]])
    left_b, right_b = along_x(middle, 1), along_x(middle, -1)
    hop_3 = round_y(other_chip)
    up4, down4, left_b, right_b, hop_3 = tie(up4, down4, left_b, right_b, hop_3)
    own = [g, up1, down1, up2[64:], down2[:64], up3[64:], down3[:64]]
    second = [far, up2[:64], down2[64:], up3[:64], down3[64:]]
    grads_early = jnp.concatenate(own + second)
    early = early_partial(grads_early, down_weight)

    up5, down5 = along_z(up4[:32], 1), along_z(down4[64:], -1)
    last = jnp.concatenate([up4[64:], down4[:32]])
    hop_4 = round_y(hop_3[:128])
    third = jnp.concatenate([up3[64:], down3[:64]])
    left_c, right_c = along_x(third, 1), along_x(third, -1)
    up5, down5, early, hop_4 = tie(up5, down5, early, hop_4)

    grads_late = jnp.concatenate([last, up4[:64], down4[32:], up5, down5])
    mine, other = late_partial(early, grads_late, down_weight)
    mine, other, left_c, right_c = tie(mine, other, left_c, right_c)
    other = swap(other, "c")
    came = jnp.concatenate([hop_1, hop_2, hop_3, hop_4])
    swapped = swap(came, "c")

    def summed(block):
        return mine[128 * block : 128 * block + 128] + other[128 * block : 128 * block + 128].astype(F32)

    to_above, to_below, to_across = summed(1).astype(BF), summed(3).astype(BF), summed(2).astype(BF)
    to_above, to_below, to_across, swapped, last = tie(to_above, to_below, to_across, swapped, last)
    left_d, right_d = along_x(last, 1), along_x(last, -1)
    from_across = along_y(to_across, 2)
    from_below, from_above = along_y(to_above, 1), along_y(to_below, -1)

    grads = jnp.concatenate(
        [grads_early[:448], last, grads_early[448:], grads_late[64:], left_a, left_b, left_c, left_d]
        + [right_a, right_b, right_c, right_d]
    )
    acts = jnp.concatenate([chip, other_chip, came, swapped])
    weight_grad = weight_gradient(grads, acts)
    from_across, from_below, from_above, weight_grad = tie(from_across, from_below, from_above, weight_grad)
    grad_act = summed(0) + from_below.astype(F32) + from_above.astype(F32) + from_across.astype(F32)
    pre_grad = (grad_act * gelu_slope(pre_wide)).astype(BF)
    return (pre_grad, weight_grad)


def solution(mesh):
    physical = Mesh(mesh.devices.reshape(XL, Y, C, XH, Z), AXES)
    rep, row, col = "xl", ("y", "c"), ("xh", "z")
    return jax.shard_map(
        per_device,
        mesh=physical,
        in_specs=(P((rep, *row), col), P((rep, *col), row), P(row, col)),
        out_specs=(P((rep, *row), col), P(row, col)),
        check_vma=False,
    )
```

```python
import jax
import jax.numpy as jnp
from jax import lax
from jax.experimental import pallas as pl
from jax.experimental.pallas import tpu as pltpu
from jax.sharding import Mesh, PartitionSpec as P

root_coef = 0.7978845608
cube_coef = 0.044715

XL, Y, C, XH, Z = 2, 4, 2, 2, 8
AXES = ("xl", "y", "c", "xh", "z")
BF, F32 = jnp.bfloat16, jnp.float32


def gelu_tanh(value):
    inner = jnp.tanh(root_coef * (value + cube_coef * value * value * value))
    return 0.5 * value * (1.0 + inner)


def gelu_slope(value):
    inner = jnp.tanh(root_coef * (value + cube_coef * value * value * value))
    return 0.5 * (1.0 + inner) + 0.5 * value * (1.0 - inner * inner) * root_coef * (
        1.0 + 3.0 * cube_coef * value * value
    )


def along_z(a, d):
    return lax.ppermute(a, "z", [(i, (i + d) % Z) for i in range(Z)])


def along_x(a, d):
    def place(x):
        return (x % 2) * XH + x // 2

    return lax.ppermute(a, ("xl", "xh"), [(place(x), place((x + d) % 4)) for x in range(4)])


def along_y(a, d):
    return lax.ppermute(a, "y", [(i, (i + d) % Y) for i in range(Y)])


def round_y(a):
    pairs = [((y, c), ((y + (1 if c == 0 else -1)) % Y, c)) for y in range(Y) for c in range(C)]
    return lax.ppermute(a, ("y", "c"), [(s[0] * C + s[1], t[0] * C + t[1]) for s, t in pairs])


def swap(a, axis):
    return lax.ppermute(a, axis, [(0, 1), (1, 0)])


def tie(*arrays):
    return lax.optimization_barrier(arrays)


OWN = [0, -1, 1, -2, 2, -3, 3, 4]


VMEM = pl.BlockSpec(memory_space=pltpu.VMEM)
EARLY = [(0, k) for k in range(7)] + [(1, k) for k in range(5)]
LATE = [(0, 7), (1, 5), (1, 6), (1, 7)]


def early_kernel(grads_ref, w_ref, out_ref):
    out_ref[...] = jnp.dot(grads_ref[...], w_ref[...], preferred_element_type=F32)


def early_partial(grads, weight):
    step = 512
    count = 64 * len(EARLY)
    return pl.pallas_call(
        early_kernel,
        grid=(1536 // step,),
        in_specs=[pl.BlockSpec((count, 1536), lambda n: (0, 0)), pl.BlockSpec((1536, step), lambda n: (0, n))],
        out_specs=pl.BlockSpec((count, step), lambda n: (0, n)),
        out_shape=jax.ShapeDtypeStruct((count, 1536), F32),
        compiler_params=pltpu.CompilerParams(vmem_limit_bytes=16 << 20),
        cost_estimate=pl.CostEstimate(flops=2 * count * 1536 * 1536, bytes_accessed=12 << 20, transcendentals=0),
    )(grads, weight)


def late_kernel(early_ref, grads_ref, w_ref, mine_ref, other_ref, late):
    y, c, xh, z = (lax.axis_index(a) for a in ("y", "c", "xh", "z"))

    def place(source, which):
        for k, (far, j) in enumerate(which):
            xp = 1 - xh if far else xh
            zp = lax.rem(z + OWN[j] + 8, 8)
            yp, cp = 2 * xp + zp // 4, lax.rem(zp // 2, 2)
            start = pl.multiple_of(lax.rem(yp + 4 - y, 4) * 128 + lax.rem(zp, 2) * 64, 64)

            @pl.when(cp == c)
            def _():
                mine_ref[pl.ds(start, 64), :] = source[64 * k : 64 * k + 64, :]

            @pl.when(cp != c)
            def _():
                other_ref[pl.ds(start, 64), :] = source[64 * k : 64 * k + 64, :].astype(BF)

    for n in range(3):
        late[:, 512 * n : 512 * n + 512] = jnp.dot(
            grads_ref[...], w_ref[:, 512 * n : 512 * n + 512], preferred_element_type=F32
        )
    place(early_ref, EARLY)
    place(late, LATE)


def late_partial(early, grads, weight):
    return pl.pallas_call(
        late_kernel,
        in_specs=[VMEM] * 3,
        out_specs=[VMEM] * 2,
        out_shape=[jax.ShapeDtypeStruct((512, 1536), F32), jax.ShapeDtypeStruct((512, 1536), BF)],
        scratch_shapes=[pltpu.VMEM((256, 1536), F32)],
        compiler_params=pltpu.CompilerParams(vmem_limit_bytes=8 << 20),
        cost_estimate=pl.CostEstimate(flops=2 * 256 * 1536 * 1536, bytes_accessed=8 << 20, transcendentals=0),
    )(early, grads, weight)


PIECES = [
    [(2 * far, OWN[j]) for far, j in EARLY],
    [(2 * far, OWN[j]) for far, j in LATE],
    *[[(dx, OWN[j]) for j in group] for dx in (3, 1) for group in ((0, 1, 2), (3, 4), (5, 6), (7,))],
]


def weight_kernel(*refs):
    pieces, acts_refs = refs[:10], refs[10:14]
    out_ref, grads, acts = refs[14:]
    y, c, xl, xh, z = (lax.axis_index(a) for a in ("y", "c", "xl", "xh", "z"))

    @pl.when(pl.program_id(0) == 0)
    def _():
        for k, (dx, dz) in enumerate(shard for piece in PIECES for shard in piece):
            xp = lax.rem(2 * xh + xl + dx, 4)
            zp = lax.rem(z + dz + 8, 8)
            dy = lax.rem(2 * (xp // 2) + zp // 4 + 4 - y, 4)
            away = lax.rem(lax.rem(zp // 2, 2) + c, 2)
            back = jnp.where(c == 0, 3, 1)
            other = dx % 2
            half = lax.rem(zp, 2) * 64

            def copy(which, block):
                acts[64 * k : 64 * k + 64, :] = acts_refs[which][pl.ds(pl.multiple_of(block * 128 + half, 64), 64), :]

            @pl.when(dy == 0)
            def _():
                copy(other, away)

            @pl.when((dy == back) | ((dy == 2) & (away == 0)))
            def _():
                copy(2, 3 * other + jnp.where(dy == 2, 2, away))

            @pl.when((dy == 4 - back) | ((dy == 2) & (away == 1)))
            def _():
                copy(3, 3 * other + jnp.where(dy == 2, 2, 1 - away))

    lanes = pl.ds(pl.multiple_of(pl.program_id(0) * 256, 256), 256)
    start = 0
    for piece, ref in zip(PIECES, pieces):
        grads[start : start + 64 * len(piece), :] = ref[:, lanes]
        start += 64 * len(piece)
    out_ref[...] = lax.dot_general(
        grads[...], acts[...], (((0,), (0,)), ((), ())), preferred_element_type=F32
    ).astype(BF)


def weight_gradient(pieces, acts):
    step = 256
    return pl.pallas_call(
        weight_kernel,
        grid=(1536 // step,),
        in_specs=[VMEM] * 14,
        out_specs=pl.BlockSpec((step, 1536), lambda m: (m, 0)),
        out_shape=jax.ShapeDtypeStruct((1536, 1536), BF),
        scratch_shapes=[pltpu.VMEM((2048, step), BF), pltpu.VMEM((2048, 1536), BF)],
        compiler_params=pltpu.CompilerParams(vmem_limit_bytes=18 << 20),
        cost_estimate=pl.CostEstimate(flops=2 * 2048 * 1536 * 1536, bytes_accessed=17 << 20, transcendentals=0),
    )(*pieces, *acts)


def per_device(pre_act, out_grad, down_weight):
    pre_wide = pre_act.astype(F32)
    g = out_grad
    activation = gelu_tanh(pre_wide).astype(BF)

    up1, down1, far = along_z(g, 1), along_z(g, -1), along_x(g, 2)
    act_c = swap(activation, "c")
    activation, act_c, up1, down1, far = tie(activation, act_c, up1, down1, far)

    up2 = along_z(jnp.concatenate([far, up1]), 1)
    down2 = along_z(jnp.concatenate([down1, far]), -1)
    other_rep = swap(activation, "xl")
    chip = jnp.concatenate([activation, act_c])
    hop_1 = round_y(chip)
    up2, down2, other_rep, hop_1 = tie(up2, down2, other_rep, hop_1)

    up3, down3 = along_z(up2, 1), along_z(down2, -1)
    near = jnp.concatenate([g, up1, down1])
    left_a, right_a = along_x(near, 1), along_x(near, -1)
    other_chip = jnp.concatenate([other_rep, swap(other_rep, "c")])
    hop_2 = round_y(hop_1[:128])
    up3, down3, left_a, right_a, other_chip, hop_2 = tie(up3, down3, left_a, right_a, other_chip, hop_2)

    up4, down4 = along_z(up3[:96], 1), along_z(down3[32:], -1)
    middle = jnp.concatenate([up2[64:], down2[:64]])
    left_b, right_b = along_x(middle, 1), along_x(middle, -1)
    hop_3 = round_y(other_chip)
    up4, down4, left_b, right_b, hop_3 = tie(up4, down4, left_b, right_b, hop_3)
    own = [g, up1, down1, up2[64:], down2[:64], up3[64:], down3[:64]]
    second = [far, up2[:64], down2[64:], up3[:64], down3[64:]]
    grads_early = jnp.concatenate(own + second)
    early = early_partial(grads_early, down_weight)

    up5, down5 = along_z(up4[:32], 1), along_z(down4[64:], -1)
    last = jnp.concatenate([up4[64:], down4[:32]])
    hop_4 = round_y(hop_3[:128])
    third = jnp.concatenate([up3[64:], down3[:64]])
    left_c, right_c = along_x(third, 1), along_x(third, -1)
    up5, down5, early, hop_4 = tie(up5, down5, early, hop_4)

    grads_late = jnp.concatenate([last, up4[:64], down4[32:], up5, down5])
    mine, other = late_partial(early, grads_late, down_weight)
    mine, other, left_c, right_c = tie(mine, other, left_c, right_c)
    other = swap(other, "c")
    came = jnp.concatenate([hop_1, hop_2, hop_3, hop_4])
    swapped = swap(came, "c")

    def summed(block):
        return mine[128 * block : 128 * block + 128] + other[128 * block : 128 * block + 128].astype(F32)

    to_above, to_below, to_across = summed(1).astype(BF), summed(3).astype(BF), summed(2).astype(BF)
    to_above, to_below, to_across, swapped, last = tie(to_above, to_below, to_across, swapped, last)
    left_d, right_d = along_x(last, 1), along_x(last, -1)
    from_across = along_y(to_across, 2)
    from_below, from_above = along_y(to_above, 1), along_y(to_below, -1)

    arrived = [left_a, left_b, left_c, left_d, right_a, right_b, right_c, right_d]
    weight_grad = weight_gradient([grads_early, grads_late, *arrived], [chip, other_chip, came, swapped])
    from_across, from_below, from_above, weight_grad = tie(from_across, from_below, from_above, weight_grad)
    grad_act = summed(0) + from_below.astype(F32) + from_above.astype(F32) + from_across.astype(F32)
    pre_grad = (grad_act * gelu_slope(pre_wide)).astype(BF)
    return (pre_grad, weight_grad)


def solution(mesh):
    physical = Mesh(mesh.devices.reshape(XL, Y, C, XH, Z), AXES)
    rep, row, col = "xl", ("y", "c"), ("xh", "z")
    return jax.shard_map(
        per_device,
        mesh=physical,
        in_specs=(P((rep, *row), col), P((rep, *col), row), P(row, col)),
        out_specs=(P((rep, *row), col), P(row, col)),
        check_vma=False,
    )
```

```python
import jax
import jax.numpy as jnp
from jax import lax
from jax.experimental import pallas as pl
from jax.experimental.pallas import tpu as pltpu
from jax.sharding import Mesh, PartitionSpec as P

root_coef = 0.7978845608
cube_coef = 0.044715

XL, Y, C, XH, Z = 2, 4, 2, 2, 8
AXES = ("xl", "y", "c", "xh", "z")
BF, F32 = jnp.bfloat16, jnp.float32


def gelu_tanh(value):
    inner = jnp.tanh(root_coef * (value + cube_coef * value * value * value))
    return 0.5 * value * (1.0 + inner)


def gelu_slope(value):
    inner = jnp.tanh(root_coef * (value + cube_coef * value * value * value))
    return 0.5 * (1.0 + inner) + 0.5 * value * (1.0 - inner * inner) * root_coef * (
        1.0 + 3.0 * cube_coef * value * value
    )


def along_z(a, d):
    return lax.ppermute(a, "z", [(i, (i + d) % Z) for i in range(Z)])


def along_x(a, d):
    def place(x):
        return (x % 2) * XH + x // 2

    return lax.ppermute(a, ("xl", "xh"), [(place(x), place((x + d) % 4)) for x in range(4)])


def along_y(a, d):
    return lax.ppermute(a, "y", [(i, (i + d) % Y) for i in range(Y)])


def round_y(a):
    pairs = [((y, c), ((y + (1 if c == 0 else -1)) % Y, c)) for y in range(Y) for c in range(C)]
    return lax.ppermute(a, ("y", "c"), [(s[0] * C + s[1], t[0] * C + t[1]) for s, t in pairs])


def swap(a, axis):
    return lax.ppermute(a, axis, [(0, 1), (1, 0)])


def tie(*arrays):
    return lax.optimization_barrier(arrays)


OWN = [0, -1, 1, -2, 2, -3, 3, 4]


VMEM = pl.BlockSpec(memory_space=pltpu.VMEM)
EARLY = [(0, k) for k in range(7)] + [(1, k) for k in range(5)]
LATE = [(0, 7), (1, 5), (1, 6), (1, 7)]


def early_kernel(grads_ref, w_ref, out_ref):
    out_ref[...] = jnp.dot(grads_ref[...], w_ref[...], preferred_element_type=F32)


def early_partial(grads, weight):
    step = 512
    count = 64 * len(EARLY)
    return pl.pallas_call(
        early_kernel,
        grid=(1536 // step,),
        in_specs=[pl.BlockSpec((count, 1536), lambda n: (0, 0)), pl.BlockSpec((1536, step), lambda n: (0, n))],
        out_specs=pl.BlockSpec((count, step), lambda n: (0, n)),
        out_shape=jax.ShapeDtypeStruct((count, 1536), F32),
        compiler_params=pltpu.CompilerParams(vmem_limit_bytes=16 << 20),
        cost_estimate=pl.CostEstimate(flops=2 * count * 1536 * 1536, bytes_accessed=12 << 20, transcendentals=0),
    )(grads, weight)


def late_kernel(early_ref, grads_ref, w_ref, mine_ref, other_ref, late):
    y, c, xh, z = (lax.axis_index(a) for a in ("y", "c", "xh", "z"))

    def place(source, which):
        for k, (far, j) in enumerate(which):
            xp = 1 - xh if far else xh
            zp = lax.rem(z + OWN[j] + 8, 8)
            yp, cp = 2 * xp + zp // 4, lax.rem(zp // 2, 2)
            start = pl.multiple_of(lax.rem(yp + 4 - y, 4) * 128 + lax.rem(zp, 2) * 64, 64)

            @pl.when(cp == c)
            def _():
                mine_ref[pl.ds(start, 64), :] = source[64 * k : 64 * k + 64, :]

            @pl.when(cp != c)
            def _():
                other_ref[pl.ds(start, 64), :] = source[64 * k : 64 * k + 64, :].astype(BF)

    for n in range(3):
        late[:, 512 * n : 512 * n + 512] = jnp.dot(
            grads_ref[...], w_ref[:, 512 * n : 512 * n + 512], preferred_element_type=F32
        )
    place(early_ref, EARLY)
    place(late, LATE)


def late_partial(early, grads, weight):
    return pl.pallas_call(
        late_kernel,
        in_specs=[VMEM] * 3,
        out_specs=[VMEM] * 2,
        out_shape=[jax.ShapeDtypeStruct((512, 1536), F32), jax.ShapeDtypeStruct((512, 1536), BF)],
        scratch_shapes=[pltpu.VMEM((256, 1536), F32)],
        compiler_params=pltpu.CompilerParams(vmem_limit_bytes=8 << 20),
        cost_estimate=pl.CostEstimate(flops=2 * 256 * 1536 * 1536, bytes_accessed=8 << 20, transcendentals=0),
    )(early, grads, weight)


PIECES = [
    [(2 * far, OWN[j]) for far, j in EARLY],
    [(2 * far, OWN[j]) for far, j in LATE],
    *[[(dx, OWN[j]) for j in group] for dx in (3, 1) for group in ((0, 1, 2), (3, 4), (5, 6), (7,))],
]


def weight_kernel(*refs):
    pieces, acts_refs = refs[:10], refs[10:14]
    out_ref, grads, acts = refs[14:]
    y, c, xl, xh, z = (lax.axis_index(a) for a in ("y", "c", "xl", "xh", "z"))

    @pl.when(pl.program_id(0) == 0)
    def _():
        for k, (dx, dz) in enumerate(shard for piece in PIECES for shard in piece):
            xp = lax.rem(2 * xh + xl + dx, 4)
            zp = lax.rem(z + dz + 8, 8)
            dy = lax.rem(2 * (xp // 2) + zp // 4 + 4 - y, 4)
            away = lax.rem(lax.rem(zp // 2, 2) + c, 2)
            back = jnp.where(c == 0, 3, 1)
            other = dx % 2
            half = lax.rem(zp, 2) * 64

            def copy(which, block):
                acts[64 * k : 64 * k + 64, :] = acts_refs[which][pl.ds(pl.multiple_of(block * 128 + half, 64), 64), :]

            @pl.when(dy == 0)
            def _():
                copy(other, away)

            @pl.when((dy == back) | ((dy == 2) & (away == 0)))
            def _():
                copy(2, 3 * other + jnp.where(dy == 2, 2, away))

            @pl.when((dy == 4 - back) | ((dy == 2) & (away == 1)))
            def _():
                copy(3, 3 * other + jnp.where(dy == 2, 2, 1 - away))

    lanes = pl.ds(pl.multiple_of(pl.program_id(0) * 256, 256), 256)
    start = 0
    for piece, ref in zip(PIECES, pieces):
        grads[start : start + 64 * len(piece), :] = ref[:, lanes]
        start += 64 * len(piece)
    out_ref[...] = lax.dot_general(
        grads[...], acts[...], (((0,), (0,)), ((), ())), preferred_element_type=F32
    ).astype(BF)


def weight_gradient(pieces, acts):
    step = 256
    return pl.pallas_call(
        weight_kernel,
        grid=(1536 // step,),
        in_specs=[VMEM] * 14,
        out_specs=pl.BlockSpec((step, 1536), lambda m: (m, 0)),
        out_shape=jax.ShapeDtypeStruct((1536, 1536), BF),
        scratch_shapes=[pltpu.VMEM((2048, step), BF), pltpu.VMEM((2048, 1536), BF)],
        compiler_params=pltpu.CompilerParams(vmem_limit_bytes=18 << 20),
        cost_estimate=pl.CostEstimate(flops=2 * 2048 * 1536 * 1536, bytes_accessed=17 << 20, transcendentals=0),
    )(*pieces, *acts)


def per_device(pre_act, out_grad, down_weight):
    pre_wide = pre_act.astype(F32)
    g = out_grad
    activation = gelu_tanh(pre_wide).astype(BF)

    up1, down1, far = along_z(g, 1), along_z(g, -1), along_x(g, 2)
    act_c = swap(activation, "c")
    hop_2 = along_y(activation, 2)
    activation, act_c, up1, down1, far = tie(activation, act_c, up1, down1, far)

    up2 = along_z(jnp.concatenate([far, up1]), 1)
    down2 = along_z(jnp.concatenate([down1, far]), -1)
    other_rep = swap(activation, "xl")
    chip = jnp.concatenate([activation, act_c])
    hop_1 = round_y(chip)
    up2, down2, other_rep, hop_1, hop_2 = tie(up2, down2, other_rep, hop_1, hop_2)

    up3, down3 = along_z(up2, 1), along_z(down2, -1)
    near = jnp.concatenate([g, up1, down1])
    left_a, right_a = along_x(near, 1), along_x(near, -1)
    hop_4 = along_y(other_rep, 2)
    other_rep, left_a, right_a = tie(other_rep, left_a, right_a)
    other_chip = jnp.concatenate([other_rep, swap(other_rep, "c")])
    up3, down3, left_a, right_a, other_chip, hop_4 = tie(up3, down3, left_a, right_a, other_chip, hop_4)

    up4, down4 = along_z(up3[:96], 1), along_z(down3[32:], -1)
    middle = jnp.concatenate([up2[64:], down2[:64]])
    left_b, right_b = along_x(middle, 1), along_x(middle, -1)
    hop_3 = round_y(other_chip)
    up4, down4 = tie(up4, down4)
    own = [g, up1, down1, up2[64:], down2[:64], up3[64:], down3[:64]]
    second = [far, up2[:64], down2[64:], up3[:64], down3[64:]]
    grads_early = jnp.concatenate(own + second)
    early = early_partial(grads_early, down_weight)

    up5, down5 = along_z(up4[:32], 1), along_z(down4[64:], -1)
    last = jnp.concatenate([up4[64:], down4[:32]])
    third = jnp.concatenate([up3[64:], down3[:64]])
    left_c, right_c = along_x(third, 1), along_x(third, -1)
    up5, down5, early, hop_3, left_b, right_b = tie(up5, down5, early, hop_3, left_b, right_b)

    grads_late = jnp.concatenate([last, up4[:64], down4[32:], up5, down5])
    mine, other = late_partial(early, grads_late, down_weight)
    mine, other, left_c, right_c = tie(mine, other, left_c, right_c)
    other = swap(other, "c")
    came = jnp.concatenate([hop_1, hop_2, hop_3, hop_4])
    swapped = swap(came, "c")

    def summed(block):
        return mine[128 * block : 128 * block + 128] + other[128 * block : 128 * block + 128].astype(F32)

    to_above, to_below, to_across = summed(1).astype(BF), summed(3).astype(BF), summed(2).astype(BF)
    to_above, to_below, to_across, swapped, last = tie(to_above, to_below, to_across, swapped, last)
    left_d, right_d = along_x(last, 1), along_x(last, -1)
    from_across = along_y(to_across, 2)
    from_below, from_above = along_y(to_above, 1), along_y(to_below, -1)

    arrived = [left_a, left_b, left_c, left_d, right_a, right_b, right_c, right_d]
    weight_grad = weight_gradient([grads_early, grads_late, *arrived], [chip, other_chip, came, swapped])
    from_across, from_below, from_above, weight_grad = tie(from_across, from_below, from_above, weight_grad)
    grad_act = summed(0) + from_below.astype(F32) + from_above.astype(F32) + from_across.astype(F32)
    pre_grad = (grad_act * gelu_slope(pre_wide)).astype(BF)
    return (pre_grad, weight_grad)


def solution(mesh):
    physical = Mesh(mesh.devices.reshape(XL, Y, C, XH, Z), AXES)
    rep, row, col = "xl", ("y", "c"), ("xh", "z")
    return jax.shard_map(
        per_device,
        mesh=physical,
        in_specs=(P((rep, *row), col), P((rep, *col), row), P(row, col)),
        out_specs=(P((rep, *row), col), P(row, col)),
        check_vma=False,
    )
```

```python
import jax
import jax.numpy as jnp
from jax import lax
from jax.experimental import pallas as pl
from jax.experimental.pallas import tpu as pltpu
from jax.sharding import Mesh, PartitionSpec as P

root_coef = 0.7978845608
cube_coef = 0.044715

XL, Y, C, XH, Z = 2, 4, 2, 2, 8
AXES = ("xl", "y", "c", "xh", "z")
BF, F32 = jnp.bfloat16, jnp.float32


def gelu_tanh(value):
    inner = jnp.tanh(root_coef * (value + cube_coef * value * value * value))
    return 0.5 * value * (1.0 + inner)


def gelu_slope(value):
    inner = jnp.tanh(root_coef * (value + cube_coef * value * value * value))
    return 0.5 * (1.0 + inner) + 0.5 * value * (1.0 - inner * inner) * root_coef * (
        1.0 + 3.0 * cube_coef * value * value
    )


def along_z(a, d):
    return lax.ppermute(a, "z", [(i, (i + d) % Z) for i in range(Z)])


def along_x(a, d):
    def place(x):
        return (x % 2) * XH + x // 2

    return lax.ppermute(a, ("xl", "xh"), [(place(x), place((x + d) % 4)) for x in range(4)])


def along_y(a, d):
    return lax.ppermute(a, "y", [(i, (i + d) % Y) for i in range(Y)])


def round_y(a):
    pairs = [((y, c), ((y + (1 if c == 0 else -1)) % Y, c)) for y in range(Y) for c in range(C)]
    return lax.ppermute(a, ("y", "c"), [(s[0] * C + s[1], t[0] * C + t[1]) for s, t in pairs])


def swap(a, axis):
    return lax.ppermute(a, axis, [(0, 1), (1, 0)])


def tie(*arrays):
    return lax.optimization_barrier(arrays)


OWN = [0, -1, 1, -2, 2, -3, 3, 4]


VMEM = pl.BlockSpec(memory_space=pltpu.VMEM)
EARLY = [(0, k) for k in range(8)] + [(1, k) for k in range(5)]
LATE = [(1, 5), (1, 6), (1, 7)]


def early_kernel(grads_ref, w_ref, out_ref):
    out_ref[...] = jnp.dot(grads_ref[...], w_ref[...], preferred_element_type=F32)


def early_partial(grads, weight):
    step = 512
    count = 64 * len(EARLY)
    return pl.pallas_call(
        early_kernel,
        grid=(1536 // step,),
        in_specs=[pl.BlockSpec((count, 1536), lambda n: (0, 0)), pl.BlockSpec((1536, step), lambda n: (0, n))],
        out_specs=pl.BlockSpec((count, step), lambda n: (0, n)),
        out_shape=jax.ShapeDtypeStruct((count, 1536), F32),
        compiler_params=pltpu.CompilerParams(vmem_limit_bytes=16 << 20),
        cost_estimate=pl.CostEstimate(flops=2 * count * 1536 * 1536, bytes_accessed=12 << 20, transcendentals=0),
    )(grads, weight)


def late_kernel(early_ref, grads_ref, w_ref, mine_ref, other_ref, late):
    y, c, xh, z = (lax.axis_index(a) for a in ("y", "c", "xh", "z"))

    def place(source, which):
        for k, (far, j) in enumerate(which):
            xp = 1 - xh if far else xh
            zp = lax.rem(z + OWN[j] + 8, 8)
            yp, cp = 2 * xp + zp // 4, lax.rem(zp // 2, 2)
            start = pl.multiple_of(lax.rem(yp + 4 - y, 4) * 128 + lax.rem(zp, 2) * 64, 64)

            @pl.when(cp == c)
            def _():
                mine_ref[pl.ds(start, 64), :] = source[64 * k : 64 * k + 64, :]

            @pl.when(cp != c)
            def _():
                other_ref[pl.ds(start, 64), :] = source[64 * k : 64 * k + 64, :].astype(BF)

    for n in range(3):
        late[:, 512 * n : 512 * n + 512] = jnp.dot(
            grads_ref[...], w_ref[:, 512 * n : 512 * n + 512], preferred_element_type=F32
        )
    place(early_ref, EARLY)
    place(late, LATE)


def late_partial(early, grads, weight):
    return pl.pallas_call(
        late_kernel,
        in_specs=[VMEM] * 3,
        out_specs=[VMEM] * 2,
        out_shape=[jax.ShapeDtypeStruct((512, 1536), F32), jax.ShapeDtypeStruct((512, 1536), BF)],
        scratch_shapes=[pltpu.VMEM((64 * len(LATE), 1536), F32)],
        compiler_params=pltpu.CompilerParams(vmem_limit_bytes=8 << 20),
        cost_estimate=pl.CostEstimate(flops=2 * 192 * 1536 * 1536, bytes_accessed=8 << 20, transcendentals=0),
    )(early, grads, weight)


PIECES = [
    [(2 * far, OWN[j]) for far, j in EARLY],
    [(2 * far, OWN[j]) for far, j in LATE],
    *[[(dx, OWN[j]) for j in group] for dx in (3, 1) for group in ((0, 1, 2), (3, 4), (7, 5, 6))],
]


def weight_kernel(*refs):
    pieces, acts_refs = refs[:8], refs[8:13]
    out_ref, grads, acts = refs[13:]
    y, c, xl, xh, z = (lax.axis_index(a) for a in ("y", "c", "xl", "xh", "z"))

    @pl.when(pl.program_id(0) == 0)
    def _():
        for k, (dx, dz) in enumerate(shard for piece in PIECES for shard in piece):
            xp = lax.rem(2 * xh + xl + dx, 4)
            zp = lax.rem(z + dz + 8, 8)
            dy = lax.rem(2 * (xp // 2) + zp // 4 + 4 - y, 4)
            away = lax.rem(lax.rem(zp // 2, 2) + c, 2)
            back = jnp.where(c == 0, 3, 1)
            other = dx % 2
            half = lax.rem(zp, 2) * 64

            def copy(which, block):
                acts[64 * k : 64 * k + 64, :] = acts_refs[which][pl.ds(pl.multiple_of(block * 128 + half, 64), 64), :]

            @pl.when(dy == 0)
            def _():
                copy(other, away)

            @pl.when((dy == back) | ((dy == 2) & (away == 0)))
            def _():
                copy(2, 3 * other + jnp.where(dy == 2, 2, away))

            @pl.when((dy == 4 - back) | ((dy == 2) & (away == 1)))
            def _():
                if other:

                    @pl.when(dy == 2)
                    def _():
                        copy(3, 3)

                    @pl.when(dy != 2)
                    def _():
                        copy(4, 1 - away)

                else:
                    copy(3, jnp.where(dy == 2, 2, 1 - away))

    lanes = pl.ds(pl.multiple_of(pl.program_id(0) * 256, 256), 256)
    start = 0
    for piece, ref in zip(PIECES, pieces):
        grads[start : start + 64 * len(piece), :] = ref[:, lanes]
        start += 64 * len(piece)
    out_ref[...] = lax.dot_general(
        grads[...], acts[...], (((0,), (0,)), ((), ())), preferred_element_type=F32
    ).astype(BF)


def weight_gradient(pieces, acts):
    step = 256
    return pl.pallas_call(
        weight_kernel,
        grid=(1536 // step,),
        in_specs=[VMEM] * 13,
        out_specs=pl.BlockSpec((step, 1536), lambda m: (m, 0)),
        out_shape=jax.ShapeDtypeStruct((1536, 1536), BF),
        scratch_shapes=[pltpu.VMEM((2048, step), BF), pltpu.VMEM((2048, 1536), BF)],
        compiler_params=pltpu.CompilerParams(vmem_limit_bytes=18 << 20),
        cost_estimate=pl.CostEstimate(flops=2 * 2048 * 1536 * 1536, bytes_accessed=17 << 20, transcendentals=0),
    )(*pieces, *acts)


def per_device(pre_act, out_grad, down_weight):
    pre_wide = pre_act.astype(F32)
    g = out_grad
    activation = gelu_tanh(pre_wide).astype(BF)

    up1, down1, far = along_z(g, 1), along_z(g, -1), along_x(g, 2)
    opposite = along_z(g, 4)
    act_c = swap(activation, "c")
    hop_2 = along_y(activation, 2)
    activation, act_c, up1, down1, far, opposite = tie(activation, act_c, up1, down1, far, opposite)

    up2 = along_z(jnp.concatenate([far, up1]), 1)
    down2 = along_z(jnp.concatenate([down1, far]), -1)
    other_rep = swap(activation, "xl")
    chip = jnp.concatenate([activation, act_c])
    near = jnp.concatenate([g, up1, down1])
    hop_1 = round_y(chip)
    other_rep, near = tie(other_rep, near)
    left_a, right_a = along_x(near, 1), along_x(near, -1)
    far_opposite = along_x(opposite, 2)
    up2, down2, other_rep, hop_1, hop_2 = tie(up2, down2, other_rep, hop_1, hop_2)

    up3, down3 = along_z(up2, 1), along_z(down2, -1)
    hop_4 = along_y(other_rep, 2)
    other_rep, left_a, right_a = tie(other_rep, left_a, right_a)
    other_chip = jnp.concatenate([other_rep, swap(other_rep, "c")])
    middle = jnp.concatenate([up2[64:], down2[:64]])
    left_b, right_b = along_x(middle, 1), along_x(middle, -1)
    up3, down3, left_a, right_a, other_chip, far_opposite = tie(
        up3, down3, left_a, right_a, other_chip, far_opposite
    )

    up4, down4 = along_z(up3[:64], 1), along_z(down3[64:], -1)
    hop_3 = round_y(other_chip)
    own = [g, up1, down1, up2[64:], down2[:64], up3[64:], down3[:64], opposite]
    second = [far, up2[:64], down2[64:], up3[:64], down3[64:]]
    grads_early = jnp.concatenate(own + second)
    early = early_partial(grads_early, down_weight)
    third = jnp.concatenate([opposite, up3[64:], down3[:64]])
    left_c, right_c = along_x(third, 1), along_x(third, -1)
    up4, down4, early, left_b, right_b, hop_4 = tie(up4, down4, early, left_b, right_b, hop_4)
    swap_a = swap(jnp.concatenate([hop_1, hop_2, hop_4]), "c")

    grads_late = jnp.concatenate([up4, down4, far_opposite])
    mine, other = late_partial(early, grads_late, down_weight)
    other, hop_3 = tie(other, hop_3)
    other = swap(other, "c")
    swap_b = swap(hop_3, "c")

    def summed(block):
        return mine[128 * block : 128 * block + 128] + other[128 * block : 128 * block + 128].astype(F32)

    to_above, to_below, to_across = summed(1).astype(BF), summed(3).astype(BF), summed(2).astype(BF)
    to_above, to_below, to_across, swap_a, swap_b = tie(to_above, to_below, to_across, swap_a, swap_b)
    from_across = along_y(to_across, 2)
    from_below, from_above = along_y(to_above, 1), along_y(to_below, -1)

    arrived = [left_a, left_b, left_c, right_a, right_b, right_c]
    came = jnp.concatenate([hop_1, hop_2, hop_3, hop_4])
    weight_grad = weight_gradient([grads_early, grads_late, *arrived], [chip, other_chip, came, swap_a, swap_b])
    from_across, from_below, from_above, weight_grad = tie(from_across, from_below, from_above, weight_grad)
    grad_act = summed(0) + from_below.astype(F32) + from_above.astype(F32) + from_across.astype(F32)
    pre_grad = (grad_act * gelu_slope(pre_wide)).astype(BF)
    return (pre_grad, weight_grad)


def solution(mesh):
    physical = Mesh(mesh.devices.reshape(XL, Y, C, XH, Z), AXES)
    rep, row, col = "xl", ("y", "c"), ("xh", "z")
    return jax.shard_map(
        per_device,
        mesh=physical,
        in_specs=(P((rep, *row), col), P((rep, *col), row), P(row, col)),
        out_specs=(P((rep, *row), col), P(row, col)),
        check_vma=False,
    )
```

```python
import jax
import jax.numpy as jnp
from jax import lax
from jax.experimental import pallas as pl
from jax.experimental.pallas import tpu as pltpu
from jax.sharding import Mesh, PartitionSpec as P

root_coef = 0.7978845608
cube_coef = 0.044715

XL, Y, C, XH, Z = 2, 4, 2, 2, 8
AXES = ("xl", "y", "c", "xh", "z")
BF, F32 = jnp.bfloat16, jnp.float32


def gelu_tanh(value):
    inner = jnp.tanh(root_coef * (value + cube_coef * value * value * value))
    return 0.5 * value * (1.0 + inner)


def gelu_slope(value):
    inner = jnp.tanh(root_coef * (value + cube_coef * value * value * value))
    return 0.5 * (1.0 + inner) + 0.5 * value * (1.0 - inner * inner) * root_coef * (
        1.0 + 3.0 * cube_coef * value * value
    )


def along_z(a, d):
    return lax.ppermute(a, "z", [(i, (i + d) % Z) for i in range(Z)])


def along_x(a, d):
    def place(x):
        return (x % 2) * XH + x // 2

    return lax.ppermute(a, ("xl", "xh"), [(place(x), place((x + d) % 4)) for x in range(4)])


def along_y(a, d):
    return lax.ppermute(a, "y", [(i, (i + d) % Y) for i in range(Y)])


def round_y(a):
    pairs = [((y, c), ((y + (1 if c == 0 else -1)) % Y, c)) for y in range(Y) for c in range(C)]
    return lax.ppermute(a, ("y", "c"), [(s[0] * C + s[1], t[0] * C + t[1]) for s, t in pairs])


def swap(a, axis):
    return lax.ppermute(a, axis, [(0, 1), (1, 0)])


def tie(*arrays):
    return lax.optimization_barrier(arrays)


OWN = [0, -1, 1, -2, 2, -3, 3, 4]


VMEM = pl.BlockSpec(memory_space=pltpu.VMEM)
EARLY = [(0, k) for k in range(7)] + [(1, k) for k in range(5)]
LATE = [(0, 7), (1, 5), (1, 6), (1, 7)]


def early_kernel(grads_ref, w_ref, out_ref):
    out_ref[...] = jnp.dot(grads_ref[...], w_ref[...], preferred_element_type=F32)


def early_partial(grads, weight):
    step = 512
    count = 64 * len(EARLY)
    return pl.pallas_call(
        early_kernel,
        grid=(1536 // step,),
        in_specs=[pl.BlockSpec((count, 1536), lambda n: (0, 0)), pl.BlockSpec((1536, step), lambda n: (0, n))],
        out_specs=pl.BlockSpec((count, step), lambda n: (0, n)),
        out_shape=jax.ShapeDtypeStruct((count, 1536), F32),
        compiler_params=pltpu.CompilerParams(vmem_limit_bytes=16 << 20),
        cost_estimate=pl.CostEstimate(flops=2 * count * 1536 * 1536, bytes_accessed=12 << 20, transcendentals=0),
    )(grads, weight)


def late_kernel(early_ref, grads_ref, w_ref, mine_ref, other_ref, late):
    y, c, xh, z = (lax.axis_index(a) for a in ("y", "c", "xh", "z"))

    def place(source, which):
        for k, (far, j) in enumerate(which):
            xp = 1 - xh if far else xh
            zp = lax.rem(z + OWN[j] + 8, 8)
            yp, cp = 2 * xp + zp // 4, lax.rem(zp // 2, 2)
            start = pl.multiple_of(lax.rem(yp + 4 - y, 4) * 128 + lax.rem(zp, 2) * 64, 64)

            @pl.when(cp == c)
            def _():
                mine_ref[pl.ds(start, 64), :] = source[64 * k : 64 * k + 64, :]

            @pl.when(cp != c)
            def _():
                other_ref[pl.ds(start, 64), :] = source[64 * k : 64 * k + 64, :].astype(BF)

    for n in range(3):
        late[:, 512 * n : 512 * n + 512] = jnp.dot(
            grads_ref[...], w_ref[:, 512 * n : 512 * n + 512], preferred_element_type=F32
        )
    place(early_ref, EARLY)
    place(late, LATE)


def late_partial(early, grads, weight):
    return pl.pallas_call(
        late_kernel,
        in_specs=[VMEM] * 3,
        out_specs=[VMEM] * 2,
        out_shape=[jax.ShapeDtypeStruct((512, 1536), F32), jax.ShapeDtypeStruct((512, 1536), BF)],
        scratch_shapes=[pltpu.VMEM((256, 1536), F32)],
        compiler_params=pltpu.CompilerParams(vmem_limit_bytes=8 << 20),
        cost_estimate=pl.CostEstimate(flops=2 * 256 * 1536 * 1536, bytes_accessed=8 << 20, transcendentals=0),
    )(early, grads, weight)


PIECES = [
    [(2 * far, OWN[j]) for far, j in EARLY],
    [(2 * far, OWN[j]) for far, j in LATE],
    *[[(dx, OWN[j]) for j in group] for dx in (3, 1) for group in ((0, 1, 2), (3, 4), (5, 6), (7,))],
]


def weight_kernel(*refs):
    pieces, acts_refs = refs[:10], refs[10:14]
    out_ref, grads, acts = refs[14:]
    y, c, xl, xh, z = (lax.axis_index(a) for a in ("y", "c", "xl", "xh", "z"))

    @pl.when(pl.program_id(0) == 0)
    def _():
        for k, (dx, dz) in enumerate(shard for piece in PIECES for shard in piece):
            xp = lax.rem(2 * xh + xl + dx, 4)
            zp = lax.rem(z + dz + 8, 8)
            dy = lax.rem(2 * (xp // 2) + zp // 4 + 4 - y, 4)
            away = lax.rem(lax.rem(zp // 2, 2) + c, 2)
            back = jnp.where(c == 0, 3, 1)
            other = dx % 2
            half = lax.rem(zp, 2) * 64

            def copy(which, block):
                acts[64 * k : 64 * k + 64, :] = acts_refs[which][pl.ds(pl.multiple_of(block * 128 + half, 64), 64), :]

            @pl.when(dy == 0)
            def _():
                copy(other, away)

            @pl.when((dy == back) | ((dy == 2) & (away == 0)))
            def _():
                copy(2, 3 * other + jnp.where(dy == 2, 2, away))

            @pl.when((dy == 4 - back) | ((dy == 2) & (away == 1)))
            def _():
                copy(3, 3 * other + jnp.where(dy == 2, 2, 1 - away))

    lanes = pl.ds(pl.multiple_of(pl.program_id(0) * 256, 256), 256)
    start = 0
    for piece, ref in zip(PIECES, pieces):
        grads[start : start + 64 * len(piece), :] = ref[:, lanes]
        start += 64 * len(piece)
    out_ref[...] = lax.dot_general(
        grads[...], acts[...], (((0,), (0,)), ((), ())), preferred_element_type=F32
    ).astype(BF)


def weight_gradient(pieces, acts):
    step = 256
    return pl.pallas_call(
        weight_kernel,
        grid=(1536 // step,),
        in_specs=[VMEM] * 14,
        out_specs=pl.BlockSpec((step, 1536), lambda m: (m, 0)),
        out_shape=jax.ShapeDtypeStruct((1536, 1536), BF),
        scratch_shapes=[pltpu.VMEM((2048, step), BF), pltpu.VMEM((2048, 1536), BF)],
        compiler_params=pltpu.CompilerParams(vmem_limit_bytes=18 << 20),
        cost_estimate=pl.CostEstimate(flops=2 * 2048 * 1536 * 1536, bytes_accessed=17 << 20, transcendentals=0),
    )(*pieces, *acts)


def per_device(pre_act, out_grad, down_weight):
    pre_wide = pre_act.astype(F32)
    g = out_grad
    activation = gelu_tanh(pre_wide).astype(BF)

    up1, down1, far = along_z(g, 1), along_z(g, -1), along_x(g, 2)
    act_c = swap(activation, "c")
    hop_2 = along_y(activation, 2)
    activation, up1, down1, far = tie(activation, up1, down1, far)

    up2 = along_z(jnp.concatenate([far, up1]), 1)
    down2 = along_z(jnp.concatenate([down1, far]), -1)
    other_rep = swap(activation, "xl")
    chip = jnp.concatenate([activation, act_c])
    near = jnp.concatenate([g, up1, down1])
    other_rep, chip, near = tie(other_rep, chip, near)
    hop_1 = round_y(chip)
    left_a, right_a = along_x(near, 1), along_x(near, -1)
    up2, down2, hop_2 = tie(up2, down2, hop_2)

    up3, down3 = along_z(up2, 1), along_z(down2, -1)
    other_rep, left_a, right_a = tie(other_rep, left_a, right_a)
    other_chip = jnp.concatenate([other_rep, swap(other_rep, "c")])
    up3, down3, left_a, right_a, other_rep, other_chip, hop_1 = tie(
        up3, down3, left_a, right_a, other_rep, other_chip, hop_1
    )

    up4, down4 = along_z(up3[:96], 1), along_z(down3[32:], -1)
    middle = jnp.concatenate([up2[64:], down2[:64]])
    left_b, right_b = along_x(middle, 1), along_x(middle, -1)
    hop_4 = along_y(other_rep, 2)
    up4, down4, other_chip = tie(up4, down4, other_chip)
    own = [g, up1, down1, up2[64:], down2[:64], up3[64:], down3[:64]]
    second = [far, up2[:64], down2[64:], up3[:64], down3[64:]]
    grads_early = jnp.concatenate(own + second)
    early = early_partial(grads_early, down_weight)

    up5, down5 = along_z(up4[:32], 1), along_z(down4[64:], -1)
    last = jnp.concatenate([up4[64:], down4[:32]])
    third = jnp.concatenate([up3[64:], down3[:64]])
    left_c, right_c = along_x(third, 1), along_x(third, -1)
    hop_3 = round_y(other_chip)
    up5, down5, early, left_b, right_b, hop_4 = tie(up5, down5, early, left_b, right_b, hop_4)

    grads_late = jnp.concatenate([last, up4[:64], down4[32:], up5, down5])
    mine, other = late_partial(early, grads_late, down_weight)
    mine, other, left_c, right_c, hop_3, last = tie(mine, other, left_c, right_c, hop_3, last)
    other = swap(other, "c")
    left_d, right_d = along_x(last, 1), along_x(last, -1)

    def summed(block):
        return mine[128 * block : 128 * block + 128] + other[128 * block : 128 * block + 128].astype(F32)

    to_above, to_below, to_across = summed(1).astype(BF), summed(3).astype(BF), summed(2).astype(BF)
    to_above, to_below, to_across, hop_3, left_d, right_d = tie(
        to_above, to_below, to_across, hop_3, left_d, right_d
    )
    came = jnp.concatenate([hop_1, hop_2, hop_3, hop_4])
    swapped = swap(came, "c")
    from_across = along_y(to_across, 2)
    from_below, from_above = along_y(to_above, 1), along_y(to_below, -1)

    arrived = [left_a, left_b, left_c, left_d, right_a, right_b, right_c, right_d]
    weight_grad = weight_gradient([grads_early, grads_late, *arrived], [chip, other_chip, came, swapped])
    from_across, from_below, from_above, weight_grad = tie(from_across, from_below, from_above, weight_grad)
    grad_act = summed(0) + from_below.astype(F32) + from_above.astype(F32) + from_across.astype(F32)
    pre_grad = (grad_act * gelu_slope(pre_wide)).astype(BF)
    return (pre_grad, weight_grad)


def solution(mesh):
    physical = Mesh(mesh.devices.reshape(XL, Y, C, XH, Z), AXES)
    rep, row, col = "xl", ("y", "c"), ("xh", "z")
    return jax.shard_map(
        per_device,
        mesh=physical,
        in_specs=(P((rep, *row), col), P((rep, *col), row), P(row, col)),
        out_specs=(P((rep, *row), col), P(row, col)),
        check_vma=False,
    )
```

```python
import functools

import jax
import jax.numpy as jnp
from jax import lax
from jax.experimental import pallas as pl
from jax.experimental.pallas import tpu as pltpu
from jax.sharding import Mesh, PartitionSpec as P

root_coef = 0.7978845608
cube_coef = 0.044715

XL, Y, C, XH, Z = 2, 4, 2, 2, 8
AXES = ("xl", "y", "c", "xh", "z")
BF, F32 = jnp.bfloat16, jnp.float32


def gelu_tanh(value):
    inner = jnp.tanh(root_coef * (value + cube_coef * value * value * value))
    return 0.5 * value * (1.0 + inner)


def gelu_slope(value):
    inner = jnp.tanh(root_coef * (value + cube_coef * value * value * value))
    return 0.5 * (1.0 + inner) + 0.5 * value * (1.0 - inner * inner) * root_coef * (
        1.0 + 3.0 * cube_coef * value * value
    )


def along_z(a, d):
    return lax.ppermute(a, "z", [(i, (i + d) % Z) for i in range(Z)])


def along_x(a, d):
    def place(x):
        return (x % 2) * XH + x // 2

    return lax.ppermute(a, ("xl", "xh"), [(place(x), place((x + d) % 4)) for x in range(4)])


def along_y(a, d):
    return lax.ppermute(a, "y", [(i, (i + d) % Y) for i in range(Y)])


def round_y(a):
    pairs = [((y, c), ((y + (1 if c == 0 else -1)) % Y, c)) for y in range(Y) for c in range(C)]
    return lax.ppermute(a, ("y", "c"), [(s[0] * C + s[1], t[0] * C + t[1]) for s, t in pairs])


def swap(a, axis):
    return lax.ppermute(a, axis, [(0, 1), (1, 0)])


def tie(*arrays):
    return lax.optimization_barrier(arrays)


OWN = [0, -1, 1, -2, 2, -3, 3, 4]


VMEM = pl.BlockSpec(memory_space=pltpu.VMEM)
EARLY = [(0, k) for k in range(7)] + [(1, k) for k in range(5)]
LATE = [(0, 7), (1, 5), (1, 6), (1, 7)]


def early_kernel(grads_ref, w_ref, out_ref):
    out_ref[...] = jnp.dot(grads_ref[...], w_ref[...], preferred_element_type=F32)


def early_partial(grads, weight):
    step = 512
    count = 64 * len(EARLY)
    return pl.pallas_call(
        early_kernel,
        grid=(1536 // step,),
        in_specs=[pl.BlockSpec((count, 1536), lambda n: (0, 0)), pl.BlockSpec((1536, step), lambda n: (0, n))],
        out_specs=pl.BlockSpec((count, step), lambda n: (0, n)),
        out_shape=jax.ShapeDtypeStruct((count, 1536), F32),
        compiler_params=pltpu.CompilerParams(vmem_limit_bytes=16 << 20),
        cost_estimate=pl.CostEstimate(flops=2 * count * 1536 * 1536, bytes_accessed=12 << 20, transcendentals=0),
    )(grads, weight)


def late_kernel(early_ref, grads_ref, w_ref, mine_ref, other_ref, late):
    y, c, xh, z = (lax.axis_index(a) for a in ("y", "c", "xh", "z"))

    def place(source, which):
        for k, (far, j) in enumerate(which):
            xp = 1 - xh if far else xh
            zp = lax.rem(z + OWN[j] + 8, 8)
            yp, cp = 2 * xp + zp // 4, lax.rem(zp // 2, 2)
            start = pl.multiple_of(lax.rem(yp + 4 - y, 4) * 128 + lax.rem(zp, 2) * 64, 64)

            @pl.when(cp == c)
            def _():
                mine_ref[pl.ds(start, 64), :] = source[64 * k : 64 * k + 64, :]

            @pl.when(cp != c)
            def _():
                other_ref[pl.ds(start, 64), :] = source[64 * k : 64 * k + 64, :].astype(BF)

    for n in range(3):
        late[:, 512 * n : 512 * n + 512] = jnp.dot(
            grads_ref[...], w_ref[:, 512 * n : 512 * n + 512], preferred_element_type=F32
        )
    place(early_ref, EARLY)
    place(late, LATE)


def late_partial(early, grads, weight):
    return pl.pallas_call(
        late_kernel,
        in_specs=[VMEM] * 3,
        out_specs=[VMEM] * 2,
        out_shape=[jax.ShapeDtypeStruct((512, 1536), F32), jax.ShapeDtypeStruct((512, 1536), BF)],
        scratch_shapes=[pltpu.VMEM((256, 1536), F32)],
        compiler_params=pltpu.CompilerParams(vmem_limit_bytes=8 << 20),
        cost_estimate=pl.CostEstimate(flops=2 * 256 * 1536 * 1536, bytes_accessed=8 << 20, transcendentals=0),
    )(early, grads, weight)


PIECES = [
    [(2 * far, OWN[j]) for far, j in EARLY],
    [(2 * far, OWN[j]) for far, j in LATE],
    *[[(dx, OWN[j]) for j in group] for group in ((0, 1, 2), (3, 4), (5, 6, 7)) for dx in (3, 1)],
]


def weight_kernel(layout, *refs):
    pieces, acts_refs = refs[: len(layout)], refs[len(layout) : len(layout) + 4]
    *sum_ref, out_ref, grads, acts = refs[len(layout) + 4 :]
    y, c, xl, xh, z = (lax.axis_index(a) for a in ("y", "c", "xl", "xh", "z"))

    @pl.when(pl.program_id(0) == 0)
    def _():
        for k, (dx, dz) in enumerate(shard for piece in layout for shard in piece):
            xp = lax.rem(2 * xh + xl + dx, 4)
            zp = lax.rem(z + dz + 8, 8)
            dy = lax.rem(2 * (xp // 2) + zp // 4 + 4 - y, 4)
            away = lax.rem(lax.rem(zp // 2, 2) + c, 2)
            back = jnp.where(c == 0, 3, 1)
            other = dx % 2
            half = lax.rem(zp, 2) * 64

            def copy(which, block):
                acts[64 * k : 64 * k + 64, :] = acts_refs[which][pl.ds(pl.multiple_of(block * 128 + half, 64), 64), :]

            @pl.when(dy == 0)
            def _():
                copy(other, away)

            @pl.when((dy == back) | ((dy == 2) & (away == 0)))
            def _():
                copy(2, 3 * other + jnp.where(dy == 2, 2, away))

            @pl.when((dy == 4 - back) | ((dy == 2) & (away == 1)))
            def _():
                copy(3, 3 * other + jnp.where(dy == 2, 2, 1 - away))

    lanes = pl.ds(pl.multiple_of(pl.program_id(0) * 256, 256), 256)
    start = 0
    for piece, ref in zip(layout, pieces):
        grads[start : start + 64 * len(piece), :] = ref[:, lanes]
        start += 64 * len(piece)
    product = lax.dot_general(grads[...], acts[...], (((0,), (0,)), ((), ())), preferred_element_type=F32)
    if sum_ref:
        product = product + sum_ref[0][...]
    out_ref[...] = product.astype(out_ref.dtype)


def weight_product(layout, pieces, acts, so_far):
    step, count = 256, 64 * sum(len(piece) for piece in layout)
    block = pl.BlockSpec((step, 1536), lambda m: (m, 0))
    last = so_far is not None
    return pl.pallas_call(
        functools.partial(weight_kernel, layout),
        grid=(1536 // step,),
        in_specs=[VMEM] * (len(pieces) + 4) + [block] * last,
        out_specs=block,
        out_shape=jax.ShapeDtypeStruct((1536, 1536), BF if last else F32),
        scratch_shapes=[pltpu.VMEM((count, step), BF), pltpu.VMEM((count, 1536), BF)],
        compiler_params=pltpu.CompilerParams(vmem_limit_bytes=18 << 20),
        cost_estimate=pl.CostEstimate(flops=2 * count * 1536 * 1536, bytes_accessed=12 << 20, transcendentals=0),
    )(*pieces, *acts, *([so_far] if last else []))


def per_device(pre_act, out_grad, down_weight):
    pre_wide = pre_act.astype(F32)
    g = out_grad
    activation = gelu_tanh(pre_wide).astype(BF)

    up1, down1, far = along_z(g, 1), along_z(g, -1), along_x(g, 2)
    act_c = swap(activation, "c")
    hop_2 = along_y(activation, 2)
    activation, up1, down1, far = tie(activation, up1, down1, far)

    up2 = along_z(jnp.concatenate([far, up1]), 1)
    down2 = along_z(jnp.concatenate([down1, far]), -1)
    other_rep = swap(activation, "xl")
    chip = jnp.concatenate([activation, act_c])
    near = jnp.concatenate([g, up1, down1])
    left_a, right_a = along_x(near, 1), along_x(near, -1)
    other_rep, chip = tie(other_rep, chip)
    hop_1 = round_y(chip)
    up2, down2, hop_2 = tie(up2, down2, hop_2)

    up3, down3 = along_z(up2, 1), along_z(down2, -1)
    other_rep, left_a, right_a = tie(other_rep, left_a, right_a)
    other_chip = jnp.concatenate([other_rep, swap(other_rep, "c")])
    up3, down3, left_a, right_a, other_rep, other_chip, hop_1 = tie(
        up3, down3, left_a, right_a, other_rep, other_chip, hop_1
    )

    up4, down4 = along_z(up3[:96], 1), along_z(down3[32:], -1)
    middle = jnp.concatenate([up2[64:], down2[:64]])
    left_b, right_b = along_x(middle, 1), along_x(middle, -1)
    hop_4 = along_y(other_rep, 2)
    up4, down4, other_chip = tie(up4, down4, other_chip)
    own = [g, up1, down1, up2[64:], down2[:64], up3[64:], down3[:64]]
    second = [far, up2[:64], down2[64:], up3[:64], down3[64:]]
    grads_early = jnp.concatenate(own + second)
    early = early_partial(grads_early, down_weight)

    up5, down5 = along_z(up4[:32], 1), along_z(down4[64:], -1)
    last = jnp.concatenate([up4[64:], down4[:32]])
    hop_3 = round_y(other_chip)
    up5, down5, early, left_b, right_b, hop_4 = tie(up5, down5, early, left_b, right_b, hop_4)

    grads_late = jnp.concatenate([last, up4[:64], down4[32:], up5, down5])
    mine, other = late_partial(early, grads_late, down_weight)
    mine, other, hop_3, last = tie(mine, other, hop_3, last)
    other = swap(other, "c")
    came = jnp.concatenate([hop_1, hop_2, hop_3, hop_4])
    swapped = swap(came, "c")
    third = jnp.concatenate([up3[64:], down3[:64], last])
    left_c, right_c = along_x(third, 1), along_x(third, -1)

    def summed(block):
        return mine[128 * block : 128 * block + 128] + other[128 * block : 128 * block + 128].astype(F32)

    to_above, to_below, to_across = summed(1).astype(BF), summed(3).astype(BF), summed(2).astype(BF)
    from_across = along_y(to_across, 2)
    from_below, from_above = along_y(to_above, 1), along_y(to_below, -1)

    acts = [chip, other_chip, came, swapped]
    weight_sum = weight_product(PIECES[:5], [grads_early, grads_late, left_a, right_a, left_b], acts, None)
    weight_grad = weight_product(PIECES[5:], [right_b, left_c, right_c], acts, weight_sum)
    from_across, from_below, from_above, weight_grad = tie(from_across, from_below, from_above, weight_grad)
    grad_act = summed(0) + from_below.astype(F32) + from_above.astype(F32) + from_across.astype(F32)
    pre_grad = (grad_act * gelu_slope(pre_wide)).astype(BF)
    return (pre_grad, weight_grad)


def solution(mesh):
    physical = Mesh(mesh.devices.reshape(XL, Y, C, XH, Z), AXES)
    rep, row, col = "xl", ("y", "c"), ("xh", "z")
    return jax.shard_map(
        per_device,
        mesh=physical,
        in_specs=(P((rep, *row), col), P((rep, *col), row), P(row, col)),
        out_specs=(P((rep, *row), col), P(row, col)),
        check_vma=False,
    )
```

```python
import functools

import jax
import jax.numpy as jnp
from jax import lax
from jax.experimental import pallas as pl
from jax.experimental.pallas import tpu as pltpu
from jax.sharding import Mesh, PartitionSpec as P

root_coef = 0.7978845608
cube_coef = 0.044715

XL, Y, C, XH, Z = 2, 4, 2, 2, 8
AXES = ("xl", "y", "c", "xh", "z")
BF, F32 = jnp.bfloat16, jnp.float32


def gelu_tanh(value):
    inner = jnp.tanh(root_coef * (value + cube_coef * value * value * value))
    return 0.5 * value * (1.0 + inner)


def gelu_slope(value):
    inner = jnp.tanh(root_coef * (value + cube_coef * value * value * value))
    return 0.5 * (1.0 + inner) + 0.5 * value * (1.0 - inner * inner) * root_coef * (
        1.0 + 3.0 * cube_coef * value * value
    )


def along_z(a, d):
    return lax.ppermute(a, "z", [(i, (i + d) % Z) for i in range(Z)])


def along_x(a, d):
    def place(x):
        return (x % 2) * XH + x // 2

    return lax.ppermute(a, ("xl", "xh"), [(place(x), place((x + d) % 4)) for x in range(4)])


def along_y(a, d):
    return lax.ppermute(a, "y", [(i, (i + d) % Y) for i in range(Y)])


def round_y(a):
    pairs = [((y, c), ((y + (1 if c == 0 else -1)) % Y, c)) for y in range(Y) for c in range(C)]
    return lax.ppermute(a, ("y", "c"), [(s[0] * C + s[1], t[0] * C + t[1]) for s, t in pairs])


def swap(a, axis):
    return lax.ppermute(a, axis, [(0, 1), (1, 0)])


def tie(*arrays):
    return lax.optimization_barrier(arrays)


OWN = [0, -1, 1, -2, 2, -3, 3, 4]


VMEM = pl.BlockSpec(memory_space=pltpu.VMEM)
EARLY = [(0, k) for k in range(7)] + [(1, k) for k in range(5)]
LATE = [(0, 7), (1, 5), (1, 6), (1, 7)]


def early_kernel(grads_ref, w_ref, out_ref):
    out_ref[...] = jnp.dot(grads_ref[...], w_ref[...], preferred_element_type=F32)


def early_partial(grads, weight):
    step = 512
    count = 64 * len(EARLY)
    return pl.pallas_call(
        early_kernel,
        grid=(1536 // step,),
        in_specs=[pl.BlockSpec((count, 1536), lambda n: (0, 0)), pl.BlockSpec((1536, step), lambda n: (0, n))],
        out_specs=pl.BlockSpec((count, step), lambda n: (0, n)),
        out_shape=jax.ShapeDtypeStruct((count, 1536), F32),
        compiler_params=pltpu.CompilerParams(vmem_limit_bytes=16 << 20),
        cost_estimate=pl.CostEstimate(flops=2 * count * 1536 * 1536, bytes_accessed=12 << 20, transcendentals=0),
    )(grads, weight)


def late_kernel(early_ref, grads_ref, w_ref, mine_ref, other_ref, late):
    y, c, xh, z = (lax.axis_index(a) for a in ("y", "c", "xh", "z"))

    def place(source, which):
        for k, (far, j) in enumerate(which):
            xp = 1 - xh if far else xh
            zp = lax.rem(z + OWN[j] + 8, 8)
            yp, cp = 2 * xp + zp // 4, lax.rem(zp // 2, 2)
            start = pl.multiple_of(lax.rem(yp + 4 - y, 4) * 128 + lax.rem(zp, 2) * 64, 64)

            @pl.when(cp == c)
            def _():
                mine_ref[pl.ds(start, 64), :] = source[64 * k : 64 * k + 64, :]

            @pl.when(cp != c)
            def _():
                other_ref[pl.ds(start, 64), :] = source[64 * k : 64 * k + 64, :].astype(BF)

    for n in range(3):
        late[:, 512 * n : 512 * n + 512] = jnp.dot(
            grads_ref[...], w_ref[:, 512 * n : 512 * n + 512], preferred_element_type=F32
        )
    place(early_ref, EARLY)
    place(late, LATE)


def late_partial(early, grads, weight):
    return pl.pallas_call(
        late_kernel,
        in_specs=[VMEM] * 3,
        out_specs=[VMEM] * 2,
        out_shape=[jax.ShapeDtypeStruct((512, 1536), F32), jax.ShapeDtypeStruct((512, 1536), BF)],
        scratch_shapes=[pltpu.VMEM((256, 1536), F32)],
        compiler_params=pltpu.CompilerParams(vmem_limit_bytes=8 << 20),
        cost_estimate=pl.CostEstimate(flops=2 * 256 * 1536 * 1536, bytes_accessed=8 << 20, transcendentals=0),
    )(early, grads, weight)


PIECES = [
    [(2 * far, OWN[j]) for far, j in EARLY],
    [(2 * far, OWN[j]) for far, j in LATE],
    *[[(dx, OWN[j]) for j in group] for group in ((0, 1, 2), (3, 4), (5, 6, 7)) for dx in (3, 1)],
]


def weight_kernel(layout, *refs):
    pieces, acts_refs = refs[: len(layout)], refs[len(layout) : len(layout) + 4]
    *sum_ref, out_ref, grads, acts = refs[len(layout) + 4 :]
    y, c, xl, xh, z = (lax.axis_index(a) for a in ("y", "c", "xl", "xh", "z"))

    @pl.when(pl.program_id(0) == 0)
    def _():
        for k, (dx, dz) in enumerate(shard for piece in layout for shard in piece):
            xp = lax.rem(2 * xh + xl + dx, 4)
            zp = lax.rem(z + dz + 8, 8)
            dy = lax.rem(2 * (xp // 2) + zp // 4 + 4 - y, 4)
            away = lax.rem(lax.rem(zp // 2, 2) + c, 2)
            back = jnp.where(c == 0, 3, 1)
            other = dx % 2
            half = lax.rem(zp, 2) * 64

            def copy(which, block):
                acts[64 * k : 64 * k + 64, :] = acts_refs[which][pl.ds(pl.multiple_of(block * 128 + half, 64), 64), :]

            @pl.when(dy == 0)
            def _():
                copy(other, away)

            @pl.when((dy == back) | ((dy == 2) & (away == 0)))
            def _():
                copy(2, 3 * other + jnp.where(dy == 2, 2, away))

            @pl.when((dy == 4 - back) | ((dy == 2) & (away == 1)))
            def _():
                copy(3, 3 * other + jnp.where(dy == 2, 2, 1 - away))

    lanes = pl.ds(pl.multiple_of(pl.program_id(0) * 256, 256), 256)
    start = 0
    for piece, ref in zip(layout, pieces):
        grads[start : start + 64 * len(piece), :] = ref[:, lanes]
        start += 64 * len(piece)
    product = lax.dot_general(grads[...], acts[...], (((0,), (0,)), ((), ())), preferred_element_type=F32)
    if sum_ref:
        product = product + sum_ref[0][...]
    out_ref[...] = product.astype(out_ref.dtype)


def weight_product(layout, pieces, acts, so_far):
    step, count = 256, 64 * sum(len(piece) for piece in layout)
    block = pl.BlockSpec((step, 1536), lambda m: (m, 0))
    last = so_far is not None
    return pl.pallas_call(
        functools.partial(weight_kernel, layout),
        grid=(1536 // step,),
        in_specs=[VMEM] * (len(pieces) + 4) + [block] * last,
        out_specs=block,
        out_shape=jax.ShapeDtypeStruct((1536, 1536), BF if last else F32),
        scratch_shapes=[pltpu.VMEM((count, step), BF), pltpu.VMEM((count, 1536), BF)],
        compiler_params=pltpu.CompilerParams(vmem_limit_bytes=18 << 20),
        cost_estimate=pl.CostEstimate(flops=2 * count * 1536 * 1536, bytes_accessed=12 << 20, transcendentals=0),
    )(*pieces, *acts, *([so_far] if last else []))


def per_device(pre_act, out_grad, down_weight):
    pre_wide = pre_act.astype(F32)
    g = out_grad
    activation = gelu_tanh(pre_wide).astype(BF)

    up1, down1, far = along_z(g, 1), along_z(g, -1), along_x(g, 2)
    act_c = swap(activation, "c")
    hop_2 = along_y(activation, 2)
    activation, up1, down1, far = tie(activation, up1, down1, far)

    up2 = along_z(jnp.concatenate([far, up1]), 1)
    down2 = along_z(jnp.concatenate([down1, far]), -1)
    other_rep = swap(activation, "xl")
    chip = jnp.concatenate([activation, act_c])
    near = jnp.concatenate([g, up1, down1])
    left_a, right_a = along_x(near, 1), along_x(near, -1)
    other_rep, chip = tie(other_rep, chip)
    up2, down2, hop_2 = tie(up2, down2, hop_2)

    up3, down3 = along_z(up2, 1), along_z(down2, -1)
    hop_4 = along_y(other_rep, 2)
    other_rep, left_a, right_a = tie(other_rep, left_a, right_a)
    other_chip = jnp.concatenate([other_rep, swap(other_rep, "c")])
    up3, down3, left_a, right_a, other_chip, hop_4 = tie(up3, down3, left_a, right_a, other_chip, hop_4)

    up4, down4 = along_z(up3[:96], 1), along_z(down3[32:], -1)
    middle = jnp.concatenate([up2[64:], down2[:64]])
    left_b, right_b = along_x(middle, 1), along_x(middle, -1)
    hops = round_y(jnp.concatenate([chip, other_chip]))
    up4, down4 = tie(up4, down4)
    own = [g, up1, down1, up2[64:], down2[:64], up3[64:], down3[:64]]
    second = [far, up2[:64], down2[64:], up3[:64], down3[64:]]
    grads_early = jnp.concatenate(own + second)
    early = early_partial(grads_early, down_weight)

    up5, down5 = along_z(up4[:32], 1), along_z(down4[64:], -1)
    last = jnp.concatenate([up4[64:], down4[:32]])
    up5, down5, early, left_b, right_b = tie(up5, down5, early, left_b, right_b)

    grads_late = jnp.concatenate([last, up4[:64], down4[32:], up5, down5])
    mine, other = late_partial(early, grads_late, down_weight)
    mine, other, hops, last = tie(mine, other, hops, last)
    other = swap(other, "c")
    other, hops = tie(other, hops)
    came = jnp.concatenate([hops[:256], hop_2, hops[256:], hop_4])
    swapped = swap(came, "c")
    third = jnp.concatenate([up3[64:], down3[:64], last])
    left_c, right_c = along_x(third, 1), along_x(third, -1)

    def summed(block):
        return mine[128 * block : 128 * block + 128] + other[128 * block : 128 * block + 128].astype(F32)

    to_above, to_below, to_across = summed(1).astype(BF), summed(3).astype(BF), summed(2).astype(BF)
    from_across = along_y(to_across, 2)
    from_below, from_above = along_y(to_above, 1), along_y(to_below, -1)

    acts = [chip, other_chip, came, swapped]
    weight_sum = weight_product(PIECES[:5], [grads_early, grads_late, left_a, right_a, left_b], acts, None)
    weight_grad = weight_product(PIECES[5:], [right_b, left_c, right_c], acts, weight_sum)
    from_across, from_below, from_above, weight_grad = tie(from_across, from_below, from_above, weight_grad)
    grad_act = summed(0) + from_below.astype(F32) + from_above.astype(F32) + from_across.astype(F32)
    pre_grad = (grad_act * gelu_slope(pre_wide)).astype(BF)
    return (pre_grad, weight_grad)


def solution(mesh):
    physical = Mesh(mesh.devices.reshape(XL, Y, C, XH, Z), AXES)
    rep, row, col = "xl", ("y", "c"), ("xh", "z")
    return jax.shard_map(
        per_device,
        mesh=physical,
        in_specs=(P((rep, *row), col), P((rep, *col), row), P(row, col)),
        out_specs=(P((rep, *row), col), P(row, col)),
        check_vma=False,
    )
```

```python
import functools

import jax
import jax.numpy as jnp
from jax import lax
from jax.experimental import pallas as pl
from jax.experimental.pallas import tpu as pltpu
from jax.sharding import Mesh, PartitionSpec as P

root_coef = 0.7978845608
cube_coef = 0.044715

XL, Y, C, XH, Z = 2, 4, 2, 2, 8
AXES = ("xl", "y", "c", "xh", "z")
BF, F32 = jnp.bfloat16, jnp.float32


def gelu_tanh(value):
    inner = jnp.tanh(root_coef * (value + cube_coef * value * value * value))
    return 0.5 * value * (1.0 + inner)


def gelu_slope(value):
    inner = jnp.tanh(root_coef * (value + cube_coef * value * value * value))
    return 0.5 * (1.0 + inner) + 0.5 * value * (1.0 - inner * inner) * root_coef * (
        1.0 + 3.0 * cube_coef * value * value
    )


def along_z(a, d):
    return lax.ppermute(a, "z", [(i, (i + d) % Z) for i in range(Z)])


def along_x(a, d):
    def place(x):
        return (x % 2) * XH + x // 2

    return lax.ppermute(a, ("xl", "xh"), [(place(x), place((x + d) % 4)) for x in range(4)])


def along_y(a, d):
    return lax.ppermute(a, "y", [(i, (i + d) % Y) for i in range(Y)])


def round_y(a):
    pairs = [((y, c), ((y + (1 if c == 0 else -1)) % Y, c)) for y in range(Y) for c in range(C)]
    return lax.ppermute(a, ("y", "c"), [(s[0] * C + s[1], t[0] * C + t[1]) for s, t in pairs])


def swap(a, axis):
    return lax.ppermute(a, axis, [(0, 1), (1, 0)])


def tie(*arrays):
    return lax.optimization_barrier(arrays)


OWN = [0, -1, 1, -2, 2, -3, 3, 4]


VMEM = pl.BlockSpec(memory_space=pltpu.VMEM)
EARLY = [(0, k) for k in range(7)] + [(1, k) for k in range(5)]
LATE = [(0, 7), (1, 5), (1, 6), (1, 7)]


def early_kernel(grads_ref, w_ref, out_ref):
    out_ref[...] = jnp.dot(grads_ref[...], w_ref[...], preferred_element_type=F32)


def early_partial(grads, weight):
    step = 512
    count = 64 * len(EARLY)
    return pl.pallas_call(
        early_kernel,
        grid=(1536 // step,),
        in_specs=[pl.BlockSpec((count, 1536), lambda n: (0, 0)), pl.BlockSpec((1536, step), lambda n: (0, n))],
        out_specs=pl.BlockSpec((count, step), lambda n: (0, n)),
        out_shape=jax.ShapeDtypeStruct((count, 1536), F32),
        compiler_params=pltpu.CompilerParams(vmem_limit_bytes=16 << 20),
        cost_estimate=pl.CostEstimate(flops=2 * count * 1536 * 1536, bytes_accessed=12 << 20, transcendentals=0),
    )(grads, weight)


def late_kernel(early_ref, grads_ref, w_ref, mine_ref, other_ref, late):
    y, c, xh, z = (lax.axis_index(a) for a in ("y", "c", "xh", "z"))

    def place(source, which):
        for k, (far, j) in enumerate(which):
            xp = 1 - xh if far else xh
            zp = lax.rem(z + OWN[j] + 8, 8)
            yp, cp = 2 * xp + zp // 4, lax.rem(zp // 2, 2)
            start = pl.multiple_of(lax.rem(yp + 4 - y, 4) * 128 + lax.rem(zp, 2) * 64, 64)

            @pl.when(cp == c)
            def _():
                mine_ref[pl.ds(start, 64), :] = source[64 * k : 64 * k + 64, :]

            @pl.when(cp != c)
            def _():
                other_ref[pl.ds(start, 64), :] = source[64 * k : 64 * k + 64, :].astype(BF)

    for n in range(3):
        late[:, 512 * n : 512 * n + 512] = jnp.dot(
            grads_ref[...], w_ref[:, 512 * n : 512 * n + 512], preferred_element_type=F32
        )
    place(early_ref, EARLY)
    place(late, LATE)


def late_partial(early, grads, weight):
    return pl.pallas_call(
        late_kernel,
        in_specs=[VMEM] * 3,
        out_specs=[VMEM] * 2,
        out_shape=[jax.ShapeDtypeStruct((512, 1536), F32), jax.ShapeDtypeStruct((512, 1536), BF)],
        scratch_shapes=[pltpu.VMEM((256, 1536), F32)],
        compiler_params=pltpu.CompilerParams(vmem_limit_bytes=8 << 20),
        cost_estimate=pl.CostEstimate(flops=2 * 256 * 1536 * 1536, bytes_accessed=8 << 20, transcendentals=0),
    )(early, grads, weight)


PIECES = [
    [(2 * far, OWN[j]) for far, j in EARLY],
    [(2 * far, OWN[j]) for far, j in LATE],
    *[[(dx, OWN[j]) for j in group] for group in ((0, 1, 2), (3, 4), (5, 6, 7)) for dx in (3, 1)],
]


def weight_kernel(layout, *refs):
    pieces, acts_refs = refs[: len(layout)], refs[len(layout) : len(layout) + 7]
    *sum_ref, out_ref, grads, acts = refs[len(layout) + 7 :]
    y, c, xl, xh, z = (lax.axis_index(a) for a in ("y", "c", "xl", "xh", "z"))

    @pl.when(pl.program_id(0) == 0)
    def _():
        for k, (dx, dz) in enumerate(shard for piece in layout for shard in piece):
            xp = lax.rem(2 * xh + xl + dx, 4)
            zp = lax.rem(z + dz + 8, 8)
            dy = lax.rem(2 * (xp // 2) + zp // 4 + 4 - y, 4)
            away = lax.rem(lax.rem(zp // 2, 2) + c, 2)
            back = jnp.where(c == 0, 3, 1)
            other = dx % 2
            half = lax.rem(zp, 2) * 64

            def copy(which, block):
                acts[64 * k : 64 * k + 64, :] = acts_refs[which][pl.ds(pl.multiple_of(block * 128 + half, 64), 64), :]

            @pl.when(dy == 0)
            def _():
                copy(other, away)

            @pl.when(dy == back)
            def _():
                copy(2, 2 * other + away)

            @pl.when(dy == 4 - back)
            def _():
                copy(3, 2 * other + 1 - away)

            @pl.when((dy == 2) & (away == 0))
            def _():
                copy(4 + other, 0)

            @pl.when((dy == 2) & (away == 1))
            def _():
                copy(6, other)

    lanes = pl.ds(pl.multiple_of(pl.program_id(0) * 256, 256), 256)
    start = 0
    for piece, ref in zip(layout, pieces):
        grads[start : start + 64 * len(piece), :] = ref[:, lanes]
        start += 64 * len(piece)
    product = lax.dot_general(grads[...], acts[...], (((0,), (0,)), ((), ())), preferred_element_type=F32)
    if sum_ref:
        product = product + sum_ref[0][...]
    out_ref[...] = product.astype(out_ref.dtype)


def weight_product(layout, pieces, acts, so_far):
    step, count = 256, 64 * sum(len(piece) for piece in layout)
    block = pl.BlockSpec((step, 1536), lambda m: (m, 0))
    last = so_far is not None
    return pl.pallas_call(
        functools.partial(weight_kernel, layout),
        grid=(1536 // step,),
        in_specs=[VMEM] * (len(pieces) + 7) + [block] * last,
        out_specs=block,
        out_shape=jax.ShapeDtypeStruct((1536, 1536), BF if last else F32),
        scratch_shapes=[pltpu.VMEM((count, step), BF), pltpu.VMEM((count, 1536), BF)],
        compiler_params=pltpu.CompilerParams(vmem_limit_bytes=18 << 20),
        cost_estimate=pl.CostEstimate(flops=2 * count * 1536 * 1536, bytes_accessed=12 << 20, transcendentals=0),
    )(*pieces, *acts, *([so_far] if last else []))


def per_device(pre_act, out_grad, down_weight):
    pre_wide = pre_act.astype(F32)
    g = out_grad
    activation = gelu_tanh(pre_wide).astype(BF)

    up1, down1, far = along_z(g, 1), along_z(g, -1), along_x(g, 2)
    act_c = swap(activation, "c")
    hop_2 = along_y(activation, 2)
    activation, up1, down1, far = tie(activation, up1, down1, far)

    up2 = along_z(jnp.concatenate([far, up1]), 1)
    down2 = along_z(jnp.concatenate([down1, far]), -1)
    other_rep = swap(activation, "xl")
    chip = jnp.concatenate([activation, act_c])
    near = jnp.concatenate([g, up1, down1])
    left_a, right_a = along_x(near, 1), along_x(near, -1)
    other_rep, chip = tie(other_rep, chip)
    up2, down2, hop_2 = tie(up2, down2, hop_2)

    up3, down3 = along_z(up2, 1), along_z(down2, -1)
    hop_4 = along_y(other_rep, 2)
    other_rep, left_a, right_a = tie(other_rep, left_a, right_a)
    other_chip = jnp.concatenate([other_rep, swap(other_rep, "c")])
    up3, down3, left_a, right_a, other_chip, hop_4 = tie(up3, down3, left_a, right_a, other_chip, hop_4)

    up4, down4 = along_z(up3[:96], 1), along_z(down3[32:], -1)
    middle = jnp.concatenate([up2[64:], down2[:64]])
    left_b, right_b = along_x(middle, 1), along_x(middle, -1)
    hops = round_y(jnp.concatenate([chip, other_chip]))
    up4, down4 = tie(up4, down4)
    own = [g, up1, down1, up2[64:], down2[:64], up3[64:], down3[:64]]
    second = [far, up2[:64], down2[64:], up3[:64], down3[64:]]
    grads_early = jnp.concatenate(own + second)
    early = early_partial(grads_early, down_weight)

    up5, down5 = along_z(up4[:32], 1), along_z(down4[64:], -1)
    last = jnp.concatenate([up4[64:], down4[:32]])
    up5, down5, early, left_b, right_b = tie(up5, down5, early, left_b, right_b)

    grads_late = jnp.concatenate([last, up4[:64], down4[32:], up5, down5])
    mine, other = late_partial(early, grads_late, down_weight)
    mine, other, hop_2, hop_4, last = tie(mine, other, hop_2, hop_4, last)
    swap_a = swap(jnp.concatenate([hop_2, hop_4]), "c")
    other, hops, swap_a = tie(other, hops, swap_a)
    other = swap(other, "c")
    other, hops = tie(other, hops)
    swap_b = swap(hops, "c")
    third = jnp.concatenate([up3[64:], down3[:64], last])
    left_c, right_c = along_x(third, 1), along_x(third, -1)

    def summed(block):
        return mine[128 * block : 128 * block + 128] + other[128 * block : 128 * block + 128].astype(F32)

    to_above, to_below, to_across = summed(1).astype(BF), summed(3).astype(BF), summed(2).astype(BF)
    from_across = along_y(to_across, 2)
    from_below, from_above = along_y(to_above, 1), along_y(to_below, -1)

    acts = [chip, other_chip, hops, swap_b, hop_2, hop_4, swap_a]
    weight_sum = weight_product(PIECES[:5], [grads_early, grads_late, left_a, right_a, left_b], acts, None)
    weight_grad = weight_product(PIECES[5:], [right_b, left_c, right_c], acts, weight_sum)
    from_across, from_below, from_above, weight_grad = tie(from_across, from_below, from_above, weight_grad)
    grad_act = summed(0) + from_below.astype(F32) + from_above.astype(F32) + from_across.astype(F32)
    pre_grad = (grad_act * gelu_slope(pre_wide)).astype(BF)
    return (pre_grad, weight_grad)


def solution(mesh):
    physical = Mesh(mesh.devices.reshape(XL, Y, C, XH, Z), AXES)
    rep, row, col = "xl", ("y", "c"), ("xh", "z")
    return jax.shard_map(
        per_device,
        mesh=physical,
        in_specs=(P((rep, *row), col), P((rep, *col), row), P(row, col)),
        out_specs=(P((rep, *row), col), P(row, col)),
        check_vma=False,
    )
```

```python
import functools

import jax
import jax.numpy as jnp
from jax import lax
from jax.experimental import pallas as pl
from jax.experimental.pallas import tpu as pltpu
from jax.sharding import Mesh, PartitionSpec as P

root_coef = 0.7978845608
cube_coef = 0.044715

XL, Y, C, XH, Z = 2, 4, 2, 2, 8
AXES = ("xl", "y", "c", "xh", "z")
BF, F32 = jnp.bfloat16, jnp.float32


def gelu_tanh(value):
    inner = jnp.tanh(root_coef * (value + cube_coef * value * value * value))
    return 0.5 * value * (1.0 + inner)


def gelu_slope(value):
    inner = jnp.tanh(root_coef * (value + cube_coef * value * value * value))
    return 0.5 * (1.0 + inner) + 0.5 * value * (1.0 - inner * inner) * root_coef * (
        1.0 + 3.0 * cube_coef * value * value
    )


def along_z(a, d):
    return lax.ppermute(a, "z", [(i, (i + d) % Z) for i in range(Z)])


def along_x(a, d):
    def place(x):
        return (x % 2) * XH + x // 2

    return lax.ppermute(a, ("xl", "xh"), [(place(x), place((x + d) % 4)) for x in range(4)])


def along_y(a, d):
    return lax.ppermute(a, "y", [(i, (i + d) % Y) for i in range(Y)])


def round_y(a):
    pairs = [((y, c), ((y + (1 if c == 0 else -1)) % Y, c)) for y in range(Y) for c in range(C)]
    return lax.ppermute(a, ("y", "c"), [(s[0] * C + s[1], t[0] * C + t[1]) for s, t in pairs])


def swap(a, axis):
    return lax.ppermute(a, axis, [(0, 1), (1, 0)])


def tie(*arrays):
    return lax.optimization_barrier(arrays)


OWN = [0, -1, 1, -2, 2, -3, 3, 4]


VMEM = pl.BlockSpec(memory_space=pltpu.VMEM)
EARLY = [(0, k) for k in range(7)] + [(1, k) for k in range(5)]
LATE = [(0, 7), (1, 5), (1, 6), (1, 7)]


def early_kernel(grads_ref, w_ref, out_ref):
    out_ref[...] = jnp.dot(grads_ref[...], w_ref[...], preferred_element_type=F32)


def early_partial(grads, weight):
    step = 512
    count = 64 * len(EARLY)
    return pl.pallas_call(
        early_kernel,
        grid=(1536 // step,),
        in_specs=[pl.BlockSpec((count, 1536), lambda n: (0, 0)), pl.BlockSpec((1536, step), lambda n: (0, n))],
        out_specs=pl.BlockSpec((count, step), lambda n: (0, n)),
        out_shape=jax.ShapeDtypeStruct((count, 1536), F32),
        compiler_params=pltpu.CompilerParams(vmem_limit_bytes=16 << 20),
        cost_estimate=pl.CostEstimate(flops=2 * count * 1536 * 1536, bytes_accessed=12 << 20, transcendentals=0),
    )(grads, weight)


def late_kernel(early_ref, grads_ref, w_ref, mine_ref, other_ref, late):
    y, c, xh, z = (lax.axis_index(a) for a in ("y", "c", "xh", "z"))

    def place(source, which):
        for k, (far, j) in enumerate(which):
            xp = 1 - xh if far else xh
            zp = lax.rem(z + OWN[j] + 8, 8)
            yp, cp = 2 * xp + zp // 4, lax.rem(zp // 2, 2)
            start = pl.multiple_of(lax.rem(yp + 4 - y, 4) * 128 + lax.rem(zp, 2) * 64, 64)

            @pl.when(cp == c)
            def _():
                mine_ref[pl.ds(start, 64), :] = source[64 * k : 64 * k + 64, :]

            @pl.when(cp != c)
            def _():
                other_ref[pl.ds(start, 64), :] = source[64 * k : 64 * k + 64, :].astype(BF)

    for n in range(3):
        late[:, 512 * n : 512 * n + 512] = jnp.dot(
            grads_ref[...], w_ref[:, 512 * n : 512 * n + 512], preferred_element_type=F32
        )
    place(early_ref, EARLY)
    place(late, LATE)


def late_partial(early, grads, weight):
    return pl.pallas_call(
        late_kernel,
        in_specs=[VMEM] * 3,
        out_specs=[VMEM] * 2,
        out_shape=[jax.ShapeDtypeStruct((512, 1536), F32), jax.ShapeDtypeStruct((512, 1536), BF)],
        scratch_shapes=[pltpu.VMEM((256, 1536), F32)],
        compiler_params=pltpu.CompilerParams(vmem_limit_bytes=8 << 20),
        cost_estimate=pl.CostEstimate(flops=2 * 256 * 1536 * 1536, bytes_accessed=8 << 20, transcendentals=0),
    )(early, grads, weight)


PIECES = [
    [(2 * far, OWN[j]) for far, j in EARLY],
    [(2 * far, OWN[j]) for far, j in LATE],
    *[[(dx, OWN[j]) for j in group] for group in ((0, 1, 2), (3, 4), (5, 6, 7)) for dx in (3, 1)],
]


def weight_kernel(layout, *refs):
    pieces, acts_refs = refs[: len(layout)], refs[len(layout) : len(layout) + 7]
    *sum_ref, out_ref, grads, acts = refs[len(layout) + 7 :]
    y, c, xl, xh, z = (lax.axis_index(a) for a in ("y", "c", "xl", "xh", "z"))

    @pl.when(pl.program_id(0) == 0)
    def _():
        for k, (dx, dz) in enumerate(shard for piece in layout for shard in piece):
            xp = lax.rem(2 * xh + xl + dx, 4)
            zp = lax.rem(z + dz + 8, 8)
            dy = lax.rem(2 * (xp // 2) + zp // 4 + 4 - y, 4)
            away = lax.rem(lax.rem(zp // 2, 2) + c, 2)
            back = jnp.where(c == 0, 3, 1)
            other = dx % 2
            half = lax.rem(zp, 2) * 64

            def copy(which, block):
                acts[64 * k : 64 * k + 64, :] = acts_refs[which][pl.ds(pl.multiple_of(block * 128 + half, 64), 64), :]

            @pl.when(dy == 0)
            def _():
                copy(other, away)

            @pl.when(dy == back)
            def _():
                copy(2, 2 * other + away)

            @pl.when(dy == 4 - back)
            def _():
                copy(3, 2 * other + 1 - away)

            @pl.when((dy == 2) & (away == 0))
            def _():
                copy(4 + other, 0)

            @pl.when((dy == 2) & (away == 1))
            def _():
                copy(6, other)

    lanes = pl.ds(pl.multiple_of(pl.program_id(0) * 256, 256), 256)
    start = 0
    for piece, ref in zip(layout, pieces):
        grads[start : start + 64 * len(piece), :] = ref[:, lanes]
        start += 64 * len(piece)
    product = lax.dot_general(grads[...], acts[...], (((0,), (0,)), ((), ())), preferred_element_type=F32)
    if sum_ref:
        out_ref[...] = (product + sum_ref[0][lanes, :]).astype(BF)
    else:
        out_ref[lanes, :] = product


def weight_product(layout, pieces, acts, so_far):
    step, count = 256, 64 * sum(len(piece) for piece in layout)
    block = pl.BlockSpec((step, 1536), lambda m: (m, 0))
    last = so_far is not None
    return pl.pallas_call(
        functools.partial(weight_kernel, layout),
        grid=(1536 // step,),
        in_specs=[VMEM] * (len(pieces) + 7 + last),
        out_specs=block if last else VMEM,
        out_shape=jax.ShapeDtypeStruct((1536, 1536), BF if last else F32),
        scratch_shapes=[pltpu.VMEM((count, step), BF), pltpu.VMEM((count, 1536), BF)],
        compiler_params=pltpu.CompilerParams(vmem_limit_bytes=18 << 20),
        cost_estimate=pl.CostEstimate(flops=2 * count * 1536 * 1536, bytes_accessed=12 << 20, transcendentals=0),
    )(*pieces, *acts, *([so_far] if last else []))


def per_device(pre_act, out_grad, down_weight):
    pre_wide = pre_act.astype(F32)
    g = out_grad
    activation = gelu_tanh(pre_wide).astype(BF)
    slope = gelu_slope(pre_wide)

    up1, down1, far = along_z(g, 1), along_z(g, -1), along_x(g, 2)
    act_c = swap(activation, "c")
    hop_2 = along_y(activation, 2)
    activation, up1, down1, far = tie(activation, up1, down1, far)

    up2 = along_z(jnp.concatenate([far, up1]), 1)
    down2 = along_z(jnp.concatenate([down1, far]), -1)
    other_rep = swap(activation, "xl")
    chip = jnp.concatenate([activation, act_c])
    near = jnp.concatenate([g, up1, down1])
    left_a, right_a = along_x(near, 1), along_x(near, -1)
    other_rep, chip = tie(other_rep, chip)
    up2, down2, hop_2, slope = tie(up2, down2, hop_2, slope)

    up3, down3 = along_z(up2, 1), along_z(down2, -1)
    hop_4 = along_y(other_rep, 2)
    other_rep, left_a, right_a = tie(other_rep, left_a, right_a)
    other_chip = jnp.concatenate([other_rep, swap(other_rep, "c")])
    up3, down3, left_a, right_a, other_chip, hop_4 = tie(up3, down3, left_a, right_a, other_chip, hop_4)

    up4, down4 = along_z(up3[:96], 1), along_z(down3[32:], -1)
    middle = jnp.concatenate([up2[64:], down2[:64]])
    left_b, right_b = along_x(middle, 1), along_x(middle, -1)
    hops = round_y(jnp.concatenate([chip, other_chip]))
    up4, down4 = tie(up4, down4)
    own = [g, up1, down1, up2[64:], down2[:64], up3[64:], down3[:64]]
    second = [far, up2[:64], down2[64:], up3[:64], down3[64:]]
    grads_early = jnp.concatenate(own + second)
    early = early_partial(grads_early, down_weight)

    up5, down5 = along_z(up4[:32], 1), along_z(down4[64:], -1)
    last = jnp.concatenate([up4[64:], down4[:32]])
    up5, down5, early, left_b, right_b = tie(up5, down5, early, left_b, right_b)

    grads_late = jnp.concatenate([last, up4[:64], down4[32:], up5, down5])
    mine, other = late_partial(early, grads_late, down_weight)
    mine, other, hop_2, hop_4, last = tie(mine, other, hop_2, hop_4, last)
    swap_a = swap(jnp.concatenate([hop_2, hop_4]), "c")
    other, hops, swap_a = tie(other, hops, swap_a)
    other = swap(other, "c")
    other, hops = tie(other, hops)
    swap_b = swap(hops, "c")
    third = jnp.concatenate([up3[64:], down3[:64], last])
    left_c, right_c = along_x(third, 1), along_x(third, -1)

    def summed(block):
        return mine[128 * block : 128 * block + 128] + other[128 * block : 128 * block + 128].astype(F32)

    to_above, to_below, to_across = summed(1).astype(BF), summed(3).astype(BF), summed(2).astype(BF)
    from_across = along_y(to_across, 2)
    from_below, from_above = along_y(to_above, 1), along_y(to_below, -1)

    acts = [chip, other_chip, hops, swap_b, hop_2, hop_4, swap_a]
    weight_sum = weight_product(PIECES[:5], [grads_early, grads_late, left_a, right_a, left_b], acts, None)
    weight_grad = weight_product(PIECES[5:], [right_b, left_c, right_c], acts, weight_sum)
    from_across, from_below, from_above, weight_grad = tie(from_across, from_below, from_above, weight_grad)
    grad_act = summed(0) + from_below.astype(F32) + from_above.astype(F32) + from_across.astype(F32)
    pre_grad = (grad_act * slope).astype(BF)
    return (pre_grad, weight_grad)


def solution(mesh):
    physical = Mesh(mesh.devices.reshape(XL, Y, C, XH, Z), AXES)
    rep, row, col = "xl", ("y", "c"), ("xh", "z")
    return jax.shard_map(
        per_device,
        mesh=physical,
        in_specs=(P((rep, *row), col), P((rep, *col), row), P(row, col)),
        out_specs=(P((rep, *row), col), P(row, col)),
        check_vma=False,
    )
```

```python
import functools

import jax
import jax.numpy as jnp
from jax import lax
from jax.experimental import pallas as pl
from jax.experimental.pallas import tpu as pltpu
from jax.sharding import Mesh, PartitionSpec as P

root_coef = 0.7978845608
cube_coef = 0.044715

XL, Y, C, XH, Z = 2, 4, 2, 2, 8
AXES = ("xl", "y", "c", "xh", "z")
BF, F32 = jnp.bfloat16, jnp.float32


def gelu_tanh(value):
    inner = jnp.tanh(root_coef * (value + cube_coef * value * value * value))
    return 0.5 * value * (1.0 + inner)


def gelu_slope(value):
    inner = jnp.tanh(root_coef * (value + cube_coef * value * value * value))
    return 0.5 * (1.0 + inner) + 0.5 * value * (1.0 - inner * inner) * root_coef * (
        1.0 + 3.0 * cube_coef * value * value
    )


def along_z(a, d):
    return lax.ppermute(a, "z", [(i, (i + d) % Z) for i in range(Z)])


def along_x(a, d):
    def place(x):
        return (x % 2) * XH + x // 2

    return lax.ppermute(a, ("xl", "xh"), [(place(x), place((x + d) % 4)) for x in range(4)])


def along_y(a, d):
    return lax.ppermute(a, "y", [(i, (i + d) % Y) for i in range(Y)])


def round_y(a):
    pairs = [((y, c), ((y + (1 if c == 0 else -1)) % Y, c)) for y in range(Y) for c in range(C)]
    return lax.ppermute(a, ("y", "c"), [(s[0] * C + s[1], t[0] * C + t[1]) for s, t in pairs])


def swap(a, axis):
    return lax.ppermute(a, axis, [(0, 1), (1, 0)])


def tie(*arrays):
    return lax.optimization_barrier(arrays)


OWN = [0, -1, 1, -2, 2, -3, 3, 4]


VMEM = pl.BlockSpec(memory_space=pltpu.VMEM)
EARLY = [(0, k) for k in range(7)] + [(1, k) for k in range(5)]
LATE = [(0, 7), (1, 5), (1, 6), (1, 7)]


def early_kernel(grads_ref, w_ref, out_ref):
    out_ref[...] = jnp.dot(grads_ref[...], w_ref[...], preferred_element_type=F32)


def early_partial(grads, weight):
    step = 512
    count = 64 * len(EARLY)
    return pl.pallas_call(
        early_kernel,
        grid=(1536 // step,),
        in_specs=[pl.BlockSpec((count, 1536), lambda n: (0, 0)), pl.BlockSpec((1536, step), lambda n: (0, n))],
        out_specs=pl.BlockSpec((count, step), lambda n: (0, n)),
        out_shape=jax.ShapeDtypeStruct((count, 1536), F32),
        compiler_params=pltpu.CompilerParams(vmem_limit_bytes=16 << 20),
        cost_estimate=pl.CostEstimate(flops=2 * count * 1536 * 1536, bytes_accessed=12 << 20, transcendentals=0),
    )(grads, weight)


def late_kernel(early_ref, grads_ref, w_ref, mine_ref, other_ref, late):
    y, c, xh, z = (lax.axis_index(a) for a in ("y", "c", "xh", "z"))

    def place(source, which):
        for k, (far, j) in enumerate(which):
            xp = 1 - xh if far else xh
            zp = lax.rem(z + OWN[j] + 8, 8)
            yp, cp = 2 * xp + zp // 4, lax.rem(zp // 2, 2)
            start = pl.multiple_of(lax.rem(yp + 4 - y, 4) * 128 + lax.rem(zp, 2) * 64, 64)

            @pl.when(cp == c)
            def _():
                mine_ref[pl.ds(start, 64), :] = source[64 * k : 64 * k + 64, :]

            @pl.when(cp != c)
            def _():
                other_ref[pl.ds(start, 64), :] = source[64 * k : 64 * k + 64, :].astype(BF)

    for n in range(3):
        late[:, 512 * n : 512 * n + 512] = jnp.dot(
            grads_ref[...], w_ref[:, 512 * n : 512 * n + 512], preferred_element_type=F32
        )
    place(early_ref, EARLY)
    place(late, LATE)


def late_partial(early, grads, weight):
    return pl.pallas_call(
        late_kernel,
        in_specs=[VMEM] * 3,
        out_specs=[VMEM] * 2,
        out_shape=[jax.ShapeDtypeStruct((512, 1536), F32), jax.ShapeDtypeStruct((512, 1536), BF)],
        scratch_shapes=[pltpu.VMEM((256, 1536), F32)],
        compiler_params=pltpu.CompilerParams(vmem_limit_bytes=8 << 20),
        cost_estimate=pl.CostEstimate(flops=2 * 256 * 1536 * 1536, bytes_accessed=8 << 20, transcendentals=0),
    )(early, grads, weight)


PIECES = [
    [(2 * far, OWN[j]) for far, j in EARLY],
    [(2 * far, OWN[j]) for far, j in LATE],
    *[[(dx, OWN[j]) for j in group] for group in ((0, 1, 2), (3, 4), (5, 6, 7)) for dx in (3, 1)],
]


def weight_kernel(layout, *refs):
    pieces, acts_refs = refs[: len(layout)], refs[len(layout) : len(layout) + 7]
    *sum_ref, out_ref, grads, acts = refs[len(layout) + 7 :]
    y, c, xl, xh, z = (lax.axis_index(a) for a in ("y", "c", "xl", "xh", "z"))

    @pl.when(pl.program_id(0) == 0)
    def _():
        for k, (dx, dz) in enumerate(shard for piece in layout for shard in piece):
            xp = lax.rem(2 * xh + xl + dx, 4)
            zp = lax.rem(z + dz + 8, 8)
            dy = lax.rem(2 * (xp // 2) + zp // 4 + 4 - y, 4)
            away = lax.rem(lax.rem(zp // 2, 2) + c, 2)
            back = jnp.where(c == 0, 3, 1)
            other = dx % 2
            half = lax.rem(zp, 2) * 64

            def copy(which, block):
                acts[64 * k : 64 * k + 64, :] = acts_refs[which][pl.ds(pl.multiple_of(block * 128 + half, 64), 64), :]

            @pl.when(dy == 0)
            def _():
                copy(other, away)

            @pl.when(dy == back)
            def _():
                copy(2, 2 * other + away)

            @pl.when(dy == 4 - back)
            def _():
                copy(3, 2 * other + 1 - away)

            @pl.when((dy == 2) & (away == 0))
            def _():
                copy(4 + other, 0)

            @pl.when((dy == 2) & (away == 1))
            def _():
                copy(6, other)

    lanes = pl.ds(pl.multiple_of(pl.program_id(0) * 256, 256), 256)
    start = 0
    for piece, ref in zip(layout, pieces):
        grads[start : start + 64 * len(piece), :] = ref[:, lanes]
        start += 64 * len(piece)
    product = lax.dot_general(grads[...], acts[...], (((0,), (0,)), ((), ())), preferred_element_type=F32)
    if sum_ref:
        out_ref[...] = (product + sum_ref[0][lanes, :]).astype(BF)
    else:
        out_ref[lanes, :] = product


def weight_product(layout, pieces, acts, so_far):
    step, count = 256, 64 * sum(len(piece) for piece in layout)
    block = pl.BlockSpec((step, 1536), lambda m: (m, 0))
    last = so_far is not None
    return pl.pallas_call(
        functools.partial(weight_kernel, layout),
        grid=(1536 // step,),
        in_specs=[VMEM] * (len(pieces) + 7 + last),
        out_specs=block if last else VMEM,
        out_shape=jax.ShapeDtypeStruct((1536, 1536), BF if last else F32),
        scratch_shapes=[pltpu.VMEM((count, step), BF), pltpu.VMEM((count, 1536), BF)],
        compiler_params=pltpu.CompilerParams(vmem_limit_bytes=18 << 20),
        cost_estimate=pl.CostEstimate(flops=2 * count * 1536 * 1536, bytes_accessed=12 << 20, transcendentals=0),
    )(*pieces, *acts, *([so_far] if last else []))


def per_device(pre_act, out_grad, down_weight):
    pre_wide = pre_act.astype(F32)
    g = out_grad
    activation = gelu_tanh(pre_wide).astype(BF)
    slope = gelu_slope(pre_wide)

    up1, down1, far = along_z(g, 1), along_z(g, -1), along_x(g, 2)
    act_c = swap(activation, "c")
    hop_2 = along_y(activation, 2)
    activation, up1, down1, far = tie(activation, up1, down1, far)

    up2 = along_z(jnp.concatenate([far, up1]), 1)
    down2 = along_z(jnp.concatenate([down1, far]), -1)
    other_rep = swap(activation, "xl")
    chip = jnp.concatenate([activation, act_c])
    near = jnp.concatenate([g, up1, down1])
    left_a, right_a = along_x(near, 1), along_x(near, -1)
    other_rep, chip = tie(other_rep, chip)
    up2, down2, hop_2, slope = tie(up2, down2, hop_2, slope)

    up3, down3 = along_z(up2, 1), along_z(down2, -1)
    hop_4 = along_y(other_rep, 2)
    other_rep, left_a, right_a = tie(other_rep, left_a, right_a)
    other_chip = jnp.concatenate([other_rep, swap(other_rep, "c")])
    up3, down3, left_a, right_a, other_chip, hop_4 = tie(up3, down3, left_a, right_a, other_chip, hop_4)

    up4, down4 = along_z(up3[:96], 1), along_z(down3[32:], -1)
    middle = jnp.concatenate([up2[64:], down2[:64]])
    left_b, right_b = along_x(middle, 1), along_x(middle, -1)
    hops = round_y(jnp.concatenate([chip, other_chip]))
    up4, down4 = tie(up4, down4)
    own = [g, up1, down1, up2[64:], down2[:64], up3[64:], down3[:64]]
    second = [far, up2[:64], down2[64:], up3[:64], down3[64:]]
    grads_early = jnp.concatenate(own + second)
    early = early_partial(grads_early, down_weight)

    up5, down5 = along_z(up4[:32], 1), along_z(down4[64:], -1)
    last = jnp.concatenate([up4[64:], down4[:32]])
    up5, down5, early, left_b, right_b = tie(up5, down5, early, left_b, right_b)

    grads_late = jnp.concatenate([last, up4[:64], down4[32:], up5, down5])
    mine, other = late_partial(early, grads_late, down_weight)
    mine, other, hop_2, hop_4, last = tie(mine, other, hop_2, hop_4, last)
    swap_a = swap(jnp.concatenate([hop_2, hop_4]), "c")
    other, hops, swap_a = tie(other, hops, swap_a)
    other = swap(other, "c")
    swap_b = swap(hops, "c")
    third = jnp.concatenate([up3[64:], down3[:64], last])
    left_c, right_c = along_x(third, 1), along_x(third, -1)

    def summed(block):
        return mine[128 * block : 128 * block + 128] + other[128 * block : 128 * block + 128].astype(F32)

    to_above, to_below, to_across = summed(1).astype(BF), summed(3).astype(BF), summed(2).astype(BF)
    from_across = along_y(to_across, 2)
    from_below, from_above = along_y(to_above, 1), along_y(to_below, -1)

    acts = [chip, other_chip, hops, swap_b, hop_2, hop_4, swap_a]
    weight_sum = weight_product(PIECES[:5], [grads_early, grads_late, left_a, right_a, left_b], acts, None)
    weight_grad = weight_product(PIECES[5:], [right_b, left_c, right_c], acts, weight_sum)
    from_across, from_below, from_above, weight_grad = tie(from_across, from_below, from_above, weight_grad)
    grad_act = summed(0) + from_below.astype(F32) + from_above.astype(F32) + from_across.astype(F32)
    pre_grad = (grad_act * slope).astype(BF)
    return (pre_grad, weight_grad)


def solution(mesh):
    physical = Mesh(mesh.devices.reshape(XL, Y, C, XH, Z), AXES)
    rep, row, col = "xl", ("y", "c"), ("xh", "z")
    return jax.shard_map(
        per_device,
        mesh=physical,
        in_specs=(P((rep, *row), col), P((rep, *col), row), P(row, col)),
        out_specs=(P((rep, *row), col), P(row, col)),
        check_vma=False,
    )
```
